512 devices in a mesh: dp: 64 (over y, x, z_lo), seq: 8 (over z_hi, core).
Axes of the slice: x: 4, y: 8, z: 8 (z_hi: 4, z_lo: 2; z = z_hi * 2 + z_lo), core: 2. Of those that a mesh axis runs over, the one named last changes fastest.
Arguments:
- queries: bfloat16 [64, 1024, 4096], P('dp', 'seq'), may hold values from -6.5 to 6.5
- resp_kv: bfloat16 [64, 1024, 2048], P('dp', 'seq'), may hold values from -6 to 6
- prompt_kv: bfloat16 [64, 128, 2048], P('dp', 'seq'), may hold values from -6 to 6
- d_out: bfloat16 [64, 1024, 4096], P('dp', 'seq'), may hold values from -6 to 6
- resp_lengths: int32 [64, 3], P('dp'), may hold values from 1 to 640, 1024 in all within a row
- prompt_home: int32 [64], P('dp'), may hold values from 0 to 63, as said below
Outputs:
- d_queries: bfloat16 [64, 1024, 4096], P('dp', 'seq')
- d_resp_kv: bfloat16 [64, 1024, 2048], P('dp', 'seq')
- d_prompt_kv: bfloat16 [64, 128, 2048], P('dp', 'seq')
The draws below stay inside these ranges and needn't reach their ends.
Inputs may be any that keep to these rules, and one draw needn't show every extreme that they name: (l - prompt_home[l]) mod 64 lies below 8, and equals 7 for learner 0.
All inputs are finite; a program needn't handle non-finite values.
Results may differ from the reference program's by a relative error of at most 0.017.
Values may be sent and summed in bfloat16 or wider, within the bound.
No kernel may reach another device: no remote copies, remote signals or barrier semaphores. Data moves between devices by JAX's collectives and lax.ppermute only.
A program may use at most 64 MiB of HBM per device.

```python
import math
import jax
import jax.numpy as jnp
import numpy as np
from jax import lax

H = 32
KVH = 8
HD = 128
ROWS = 128
PLEN_DEV = 16
RESP = 3
SPREAD = 8
RL = 640
LROWS = 1024
PLEN = 128
N_DP = 64
N_SEQ = 8


def draw_queries(key, part):
    key = jax.random.fold_in(key, 11)
    shape = (N_DP, N_SEQ * ROWS, H * HD)
    values = jnp.clip(jax.random.normal(key, shape, jnp.float32), -6.5, 6.5)
    return values.astype(jnp.bfloat16)


def draw_prompt_kv(key, part):
    key = jax.random.fold_in(key, 23)
    shape = (N_DP, N_SEQ * PLEN_DEV, 2 * KVH * HD)
    values = jnp.clip(jax.random.normal(key, shape, jnp.float32), -6.0, 6.0)
    return values.astype(jnp.bfloat16)


def draw_prompt_home(key, part):
    key = jax.random.fold_in(key, 37)
    learners = jnp.arange(N_DP, dtype=jnp.int32)
    offsets = jax.random.randint(key, (N_DP,), 0, SPREAD, dtype=jnp.int32)
    offsets = jnp.where(learners == 0, SPREAD - 1, offsets)
    return jnp.mod(learners - offsets, N_DP).astype(jnp.int32)


def block_levels(stream_key, extent, split, smallest, largest):
    def one(axis_at, blocks):
        draws = jax.random.uniform(jax.random.fold_in(jax.random.fold_in(stream_key, 6), axis_at), (blocks,), jnp.float32, smallest / len(split), largest / len(split))
        return jnp.repeat(jnp.exp(draws), extent[axis_at] // blocks).reshape((-1,) + (1,) * (len(extent) - axis_at - 1))

    factor_of = one(*split[0])
    for cut in split[1:]:
        factor_of = factor_of * one(*cut)
    return factor_of


def split_up(number_of, total, bound, skew):
    portions = [(1 << 20) // math.isqrt(standing ** skew) + 1 for standing in range(2, number_of + 1)]
    spare, holding = total - bound - (number_of - 1), [1] * (number_of - 1)
    while spare > 0:
        free = [i for i in range(number_of - 1) if holding[i] < bound]
        mass, left = sum([portions[i] for i in free]), spare
        for i in free:
            extra = min(bound - holding[i], max(1, left * portions[i] // mass), spare)
            holding[i] = holding[i] + extra
            spare = spare - extra
    return np.array([bound] + holding)


def uneven(own_key, count, total, reach, lean):
    if count == 2:
        one = jax.random.randint(own_key, (), max(1, total - reach), min(reach, total - 1) + 1)
        return jnp.stack([one, total - one])
    tallies = jnp.asarray(split_up(count, total, reach, lean), jnp.int32)
    twos = (count - 1) // 2
    source_of, receiver = tallies[1:1 + 2 * twos:2], tallies[2:2 + 2 * twos:2]
    margin = jnp.minimum(source_of - 1, reach - receiver)
    moved = jax.random.randint(jax.random.fold_in(own_key, 1), (twos,), 0, 1 << 20) % (margin + 1)
    tallies = tallies.at[1:1 + 2 * twos:2].set(source_of - moved).at[2:2 + 2 * twos:2].set(receiver + moved)
    return tallies[jax.random.permutation(jax.random.fold_in(own_key, 2), count)]


def bell_draw(own_key, shape, scale, reach, pieces=(), kind=jnp.bfloat16):
    entries = jax.random.normal(own_key, shape, jnp.float32) * scale
    if len(pieces) > 0:
        entries = block_levels(own_key, shape, pieces, -0.22, 0.18) * entries
    return jnp.clip(entries, min=-reach, max=reach).astype(kind)


def setup_inputs(seed: int = 0) -> dict:
    key_list = jax.random.split(jax.random.key(seed), 7)
    return {
        "queries": draw_queries(jax.random.fold_in(key_list[6], 71), 0),
        "resp_kv": bell_draw(key_list[1], (N_DP, LROWS, 2 * KVH * HD), 1.0, 6.0, ((0, 64), (1, 8))),
        "prompt_kv": draw_prompt_kv(jax.random.fold_in(key_list[6], 71), 0),
        "d_out": bell_draw(key_list[3], (N_DP, LROWS, H * HD), 1.0, 6.0, ((0, 64), (1, 8))),
        "resp_lengths": jax.vmap(lambda own: uneven(own, RESP, LROWS, RL, 2))(jax.random.split(key_list[4], N_DP)).reshape((N_DP, RESP)).astype(jnp.int32),
        "prompt_home": draw_prompt_home(jax.random.fold_in(key_list[6], 71), 0),
    }


def attend(q_rows, grad_rows, keys_all, visible):
    count = q_rows.shape[0]
    total = keys_all.shape[0]
    group = H // KVH
    scale = HD ** -0.5
    qg = q_rows.reshape(count, KVH, group, HD).transpose(1, 0, 2, 3)
    dg = grad_rows.reshape(count, KVH, group, HD).transpose(1, 0, 2, 3)
    keys = keys_all[:, :KVH * HD].reshape(total, KVH, HD).transpose(1, 0, 2)
    values = keys_all[:, KVH * HD:].reshape(total, KVH, HD).transpose(1, 0, 2)

    def one_head(operands):
        qh, dh, kh, vh = operands
        qf = qh.astype(jnp.float32)
        df = dh.astype(jnp.float32)
        kf = kh.astype(jnp.float32)
        vf = vh.astype(jnp.float32)
        scores = jnp.einsum('rgd,kd->grk', qf, kf) * scale
        scores = jnp.where(visible[None], scores, -1e30)
        top = jnp.max(scores, axis=-1, keepdims=True)
        expo = jnp.exp(scores - top)
        weights = expo / jnp.sum(expo, axis=-1, keepdims=True)
        weights_b = weights.astype(jnp.bfloat16)
        wf = weights_b.astype(jnp.float32)
        out = jnp.einsum('grk,kd->rgd', wf, vf).astype(jnp.bfloat16)
        delta = jnp.sum(df * out.astype(jnp.float32), axis=-1).T
        d_weights = jnp.einsum('rgd,kd->grk', df, vf)
        d_scores = (scale * weights * (d_weights - delta[:, :, None])).astype(jnp.bfloat16)
        sf = d_scores.astype(jnp.float32)
        d_query = jnp.einsum('grk,kd->rgd', sf, kf)
        d_key = jnp.einsum('grk,rgd->kd', sf, qf)
        d_value = jnp.einsum('grk,rgd->kd', wf, df)
        return d_query, d_key, d_value

    d_query, d_key, d_value = lax.map(one_head, (qg, dg, keys, values))
    d_query = d_query.transpose(1, 0, 2, 3).reshape(count, H * HD).astype(jnp.bfloat16)
    d_key = d_key.transpose(1, 0, 2).reshape(total, KVH * HD)
    d_value = d_value.transpose(1, 0, 2).reshape(total, KVH * HD)
    return d_query, jnp.concatenate([d_key, d_value], axis=1)


def reference(queries, resp_kv, prompt_kv, d_out, resp_lengths, prompt_home):
    span = (5 * N_SEQ) // 8
    window = (span + 1) * ROWS
    lrows = N_SEQ * ROWS
    columns = 2 * KVH * HD

    def learner(operands):
        q_all, kv_all, grad_all, lengths, home = operands
        prompt = lax.dynamic_index_in_dim(prompt_kv, home, 0, keepdims=False)
        starts = jnp.cumsum(lengths) - lengths
        row_ids = jnp.arange(lrows, dtype=jnp.int32)
        start_of = jnp.max(jnp.where(starts[None, :] <= row_ids[:, None], starts[None, :], 0), axis=1).astype(jnp.int32)
        padded = jnp.concatenate([jnp.zeros((span * ROWS, columns), kv_all.dtype), kv_all], axis=0)

        def block(carry, index):
            acc, prompt_acc = carry
            first = (index * ROWS).astype(jnp.int32)
            q_rows = lax.dynamic_slice_in_dim(q_all, first, ROWS, 0)
            grad_rows = lax.dynamic_slice_in_dim(grad_all, first, ROWS, 0)
            near = lax.dynamic_slice_in_dim(padded, first, window, 0)
            q_ids = first + jnp.arange(ROWS, dtype=jnp.int32)
            k_ids = first - span * ROWS + jnp.arange(window, dtype=jnp.int32)
            q_start = lax.dynamic_slice_in_dim(start_of, first, ROWS, 0)
            near_seen = (k_ids[None, :] >= q_start[:, None]) & (k_ids[None, :] <= q_ids[:, None])
            visible = jnp.concatenate([jnp.ones((ROWS, PLEN), bool), near_seen], axis=1)
            d_query, d_kv = attend(q_rows, grad_rows, jnp.concatenate([prompt, near], axis=0), visible)
            prompt_acc = prompt_acc + d_kv[:PLEN]
            rounded = lax.optimization_barrier(d_kv[PLEN:].astype(jnp.bfloat16)).astype(jnp.float32)
            current = lax.dynamic_slice_in_dim(acc, first, window, 0)
            acc = lax.dynamic_update_slice_in_dim(acc, current + rounded, first, 0)
            return (acc, prompt_acc), d_query

        init = (jnp.zeros((span * ROWS + lrows, columns), jnp.float32), jnp.zeros((PLEN, columns), jnp.float32))
        (acc, prompt_acc), d_queries = lax.scan(block, init, jnp.arange(N_SEQ, dtype=jnp.int32))
        return d_queries.reshape(lrows, H * HD), acc[span * ROWS:].astype(jnp.bfloat16), prompt_acc

    d_queries, d_resp, prompt_parts = lax.map(learner, (queries, resp_kv, d_out, resp_lengths, prompt_home))
    d_prompt = jax.ops.segment_sum(prompt_parts, prompt_home, num_segments=N_DP).astype(jnp.bfloat16)
    return (d_queries, d_resp, d_prompt)
```

```python
import functools

import jax
import jax.numpy as jnp
from jax import lax
from jax.experimental import pallas as pl
from jax.experimental.pallas import tpu as pltpu
from jax.sharding import PartitionSpec as P

KVH = 8
HD = 128
SPREAD = 8
NEG = -1e30
LOG2E = 1.4426950408889634


def passed_along(value, axis, by):
    peers = lax.axis_size(axis)
    return lax.ppermute(value, axis, [(i, (i + by) % peers) for i in range(peers)])


def stacked(block):
    heads = block.shape[1] // HD
    return jnp.concatenate([block[:, h * HD : (h + 1) * HD] for h in range(heads)], axis=0)


def attention_kernel(span, info, q_ref, g_ref, k_ref, v_ref, pk_ref, pv_ref, start_ref,
                     dq_ref, dk_ref, dv_ref, dpk_ref, dpv_ref, bias):
    rows = q_ref.shape[0]
    heads = q_ref.shape[1] // HD
    plen = pk_ref.shape[0]
    window = (span + 1) * rows
    scale = HD ** -0.5
    first = pl.multiple_of(info[0], rows)
    own = info[1]

    @pl.when(pl.program_id(0) == 0)
    def _():
        k_ids = first + lax.broadcasted_iota(jnp.int32, (window, rows), 0)
        q_ids = own + lax.broadcasted_iota(jnp.int32, (window, rows), 1)
        seen = (k_ids >= start_ref[...]) & (k_ids <= q_ids)
        bias[...] = jnp.where(seen, 0.0, NEG)

    near = pl.ds(first, window)
    keys = jnp.concatenate([pk_ref[...], k_ref[near, :]], axis=0)
    values = jnp.concatenate([pv_ref[...], v_ref[near, :]], axis=0)
    q_rows = stacked(q_ref[...])
    g_rows = stacked(g_ref[...])
    nt = (((1,), (1,)), ((), ()))
    nn = (((1,), (0,)), ((), ()))
    tn = (((0,), (0,)), ((), ()))
    scores = lax.dot_general(keys, q_rows, nt, preferred_element_type=jnp.float32)
    shade = jnp.concatenate([bias[...]] * heads, axis=1)
    scores = jnp.concatenate([scores[:plen], scores[plen:] + shade], axis=0)
    top = jnp.max(scores, axis=0, keepdims=True)
    expo = jnp.exp2((scores - top) * (scale * LOG2E))
    weights = expo * (1.0 / jnp.sum(expo, axis=0, keepdims=True))
    d_weights = lax.dot_general(values, g_rows, nt, preferred_element_type=jnp.float32)
    delta = jnp.sum(weights * d_weights, axis=0, keepdims=True)
    d_scores = (weights * (d_weights - delta)).astype(jnp.bfloat16)
    weights_b = weights.astype(jnp.bfloat16)
    d_value = lax.dot_general(weights_b, g_rows, nn, preferred_element_type=jnp.float32)
    d_key = lax.dot_general(d_scores, q_rows, nn, preferred_element_type=jnp.float32) * scale
    d_query = lax.dot_general(d_scores, keys, tn, preferred_element_type=jnp.float32) * scale
    d_query = d_query.astype(jnp.bfloat16)
    for h in range(heads):
        dq_ref[:, h * HD : (h + 1) * HD] = d_query[h * rows : (h + 1) * rows]
    dpk_ref[...] = d_key[:plen].astype(dpk_ref.dtype)
    dpv_ref[...] = d_value[:plen].astype(dpv_ref.dtype)
    dk_ref[...] = jnp.zeros_like(dk_ref)
    dv_ref[...] = jnp.zeros_like(dv_ref)
    dk_ref[near, :] = d_key[plen:].astype(dk_ref.dtype)
    dv_ref[near, :] = d_value[plen:].astype(dv_ref.dtype)


def attend(q_rows, grad_rows, kv, prompt, q_start, first, own, span):
    rows, columns = q_rows.shape
    total = kv.shape[0]
    plen = prompt.shape[0]
    group = columns // KVH
    half = KVH * HD
    info = jnp.stack([first, own]).astype(jnp.int32)
    bf16 = jnp.bfloat16
    at = lambda n, col: pl.BlockSpec((n, col), lambda g, s: (0, g))
    later = lambda n: pl.BlockSpec((n, HD), lambda g, s: (0, KVH + g))
    pairs = (span + 1) * rows + plen
    return pl.pallas_call(
        functools.partial(attention_kernel, span),
        grid_spec=pltpu.PrefetchScalarGridSpec(
            num_scalar_prefetch=1,
            grid=(KVH,),
            in_specs=[
                at(rows, group),
                at(rows, group),
                at(total, HD),
                later(total),
                at(plen, HD),
                later(plen),
                pl.BlockSpec((1, rows), lambda g, s: (0, 0)),
            ],
            out_specs=[
                at(rows, group),
                at(total, HD),
                at(total, HD),
                at(plen, HD),
                at(plen, HD),
            ],
            scratch_shapes=[pltpu.VMEM(((span + 1) * rows, rows), jnp.float32)],
        ),
        out_shape=[
            jax.ShapeDtypeStruct((rows, columns), bf16),
            jax.ShapeDtypeStruct((total, half), bf16),
            jax.ShapeDtypeStruct((total, half), bf16),
            jax.ShapeDtypeStruct((plen, half), bf16),
            jax.ShapeDtypeStruct((plen, half), bf16),
        ],
        compiler_params=pltpu.CompilerParams(vmem_limit_bytes=48 * 1024 * 1024),
        cost_estimate=pl.CostEstimate(
            flops=10 * rows * columns * pairs,
            bytes_accessed=12 * 1024 * 1024,
            transcendentals=rows * columns * pairs // HD,
        ),
    )(info, q_rows, grad_rows, kv, kv, prompt, prompt, q_start[None])


def on_device(queries, resp_kv, prompt_kv, d_out, resp_lengths, prompt_home):
    q_rows = queries[0]
    own_kv = resp_kv[0]
    own_prompt = prompt_kv[0]
    grad_rows = d_out[0]
    rows = q_rows.shape[0]
    n_seq = lax.axis_size("seq")
    n_dp = lax.axis_size("dp")
    span = 5 * n_seq // 8
    me_seq = lax.axis_index("seq")
    me_dp = lax.axis_index("dp")
    offset = jnp.mod(me_dp - prompt_home[0], n_dp)

    kv = lax.all_gather(own_kv, "seq", axis=0, tiled=True)

    window = own_prompt[None]
    reach = 1
    while reach < SPREAD:
        window = jnp.concatenate([window, passed_along(window, "dp", reach)], axis=0)
        reach *= 2
    chosen = lax.dynamic_index_in_dim(window, offset, 0, keepdims=False)
    prompt = lax.all_gather(chosen, "seq", axis=0, tiled=True)

    lengths = resp_lengths[0]
    starts = jnp.cumsum(lengths) - lengths
    own = me_seq * rows
    q_ids = own + jnp.arange(rows, dtype=jnp.int32)
    q_start = jnp.max(jnp.where(starts[None, :] <= q_ids[:, None], starts[None, :], 0), axis=1)
    first = jnp.maximum(me_seq - span, 0) * rows
    d_query, d_key, d_value, d_pkey, d_pvalue = attend(
        q_rows, grad_rows, kv, prompt, q_start, first, own, span
    )

    prompt_grad = lax.psum_scatter(
        jnp.concatenate([d_pkey, d_pvalue], axis=1), "seq", scatter_dimension=0, tiled=True
    )
    d_kv = lax.psum_scatter(
        jnp.concatenate([d_key, d_value], axis=1), "seq", scatter_dimension=0, tiled=True
    )

    slots = jnp.arange(SPREAD, dtype=jnp.int32)[:, None, None]
    held = jnp.where(slots == offset, prompt_grad[None], jnp.zeros((), prompt_grad.dtype))
    reach = SPREAD // 2
    while reach > 0:
        arrived = passed_along(held[reach:], "dp", -reach)
        held = (held[:reach].astype(jnp.float32) + arrived.astype(jnp.float32)).astype(held.dtype)
        reach //= 2
    return (d_query[None], d_kv[None], held)


def solution(mesh):
    placed = (
        P("dp", "seq", None),
        P("dp", "seq", None),
        P("dp", "seq", None),
        P("dp", "seq", None),
        P("dp", None),
        P("dp"),
    )
    return jax.shard_map(
        on_device,
        mesh=mesh,
        in_specs=placed,
        out_specs=(P("dp", "seq", None), P("dp", "seq", None), P("dp", "seq", None)),
        check_vma=False,
    )
```

```python
import functools

import jax
import jax.numpy as jnp
from jax import lax
from jax.experimental import pallas as pl
from jax.experimental.pallas import tpu as pltpu
from jax.sharding import PartitionSpec as P

KVH = 8
HD = 128
SPREAD = 8
NEG = -1e30
LOG2E = 1.4426950408889634


def passed_along(value, axis, by):
    peers = lax.axis_size(axis)
    return lax.ppermute(value, axis, [(i, (i + by) % peers) for i in range(peers)])


def stacked(block):
    heads = block.shape[1] // HD
    return jnp.concatenate([block[:, h * HD : (h + 1) * HD] for h in range(heads)], axis=0)


def attention_kernel(span, info, q_ref, g_ref, k_ref, v_ref, pk_ref, pv_ref, start_ref,
                     dq_ref, keep_ref, give_ref, dp_ref, bias):
    rows = q_ref.shape[0]
    heads = q_ref.shape[1] // HD
    plen = pk_ref.shape[0]
    half = KVH * HD
    window = (span + 1) * rows
    scale = HD ** -0.5
    me = info[0]
    head = pl.program_id(0)

    @pl.when(head == 0)
    def _():
        own = me * rows
        k_ids = own - span * rows + lax.broadcasted_iota(jnp.int32, (window, rows), 0)
        q_ids = own + lax.broadcasted_iota(jnp.int32, (window, rows), 1)
        seen = (k_ids >= start_ref[...]) & (k_ids <= q_ids)
        bias[...] = jnp.where(seen, 0.0, NEG)

    near = [
        pl.ds(pl.multiple_of(jnp.maximum(me - back, 0) * rows, rows), rows)
        for back in range(span, -1, -1)
    ]
    keys = jnp.concatenate([pk_ref[...]] + [k_ref[at, :] for at in near], axis=0)
    values = jnp.concatenate([pv_ref[...]] + [v_ref[at, :] for at in near], axis=0)
    q_rows = stacked(q_ref[...])
    g_rows = stacked(g_ref[...])
    nt = (((1,), (1,)), ((), ()))
    nn = (((1,), (0,)), ((), ()))
    tn = (((0,), (0,)), ((), ()))
    scores = lax.dot_general(keys, q_rows, nt, preferred_element_type=jnp.float32)
    shade = jnp.concatenate([bias[...]] * heads, axis=1)
    scores = jnp.concatenate([scores[:plen], scores[plen:] + shade], axis=0)
    top = jnp.max(scores, axis=0, keepdims=True)
    expo = jnp.exp2((scores - top) * (scale * LOG2E))
    weights = expo * (1.0 / jnp.sum(expo, axis=0, keepdims=True))
    d_weights = lax.dot_general(values, g_rows, nt, preferred_element_type=jnp.float32)
    delta = jnp.sum(weights * d_weights, axis=0, keepdims=True)
    d_scores = (weights * (d_weights - delta)).astype(jnp.bfloat16)
    weights_b = weights.astype(jnp.bfloat16)
    d_value = lax.dot_general(weights_b, g_rows, nn, preferred_element_type=jnp.float32)
    d_key = lax.dot_general(d_scores, q_rows, nn, preferred_element_type=jnp.float32) * scale
    d_query = lax.dot_general(d_scores, keys, tn, preferred_element_type=jnp.float32) * scale
    d_query = d_query.astype(jnp.bfloat16)
    for h in range(heads):
        dq_ref[:, h * HD : (h + 1) * HD] = d_query[h * rows : (h + 1) * rows]
    for part, base in ((d_key, 0), (d_value, half)):
        part = part.astype(jnp.bfloat16)
        columns = pl.ds(pl.multiple_of(base + head * HD, HD), HD)
        dp_ref[:, columns] = part[:plen]
        for back in range(span + 1):
            block = part[plen + (span - back) * rows : plen + (span - back + 1) * rows]
            into = (keep_ref, give_ref)[back % 2]
            into[back // 2, :, columns] = block


def attend(q_rows, grad_rows, kv, prompt, q_start, me, span):
    rows, columns = q_rows.shape
    total, width = kv.shape
    plen = prompt.shape[0]
    group = columns // KVH
    bf16 = jnp.bfloat16
    at = lambda n, col: pl.BlockSpec((n, col), lambda g, s: (0, g))
    later = lambda n: pl.BlockSpec((n, HD), lambda g, s: (0, KVH + g))
    pairs = (span + 1) * rows + plen
    kept, given = span // 2 + 1, (span + 1) // 2
    return pl.pallas_call(
        functools.partial(attention_kernel, span),
        grid_spec=pltpu.PrefetchScalarGridSpec(
            num_scalar_prefetch=1,
            grid=(KVH,),
            in_specs=[
                at(rows, group),
                at(rows, group),
                at(total, HD),
                later(total),
                at(plen, HD),
                later(plen),
                pl.BlockSpec((1, rows), lambda g, s: (0, 0)),
            ],
            out_specs=[
                at(rows, group),
                pl.BlockSpec((kept, rows, width), lambda g, s: (0, 0, 0)),
                pl.BlockSpec((given, rows, width), lambda g, s: (0, 0, 0)),
                pl.BlockSpec((plen, width), lambda g, s: (0, 0)),
            ],
            scratch_shapes=[pltpu.VMEM(((span + 1) * rows, rows), jnp.float32)],
        ),
        out_shape=[
            jax.ShapeDtypeStruct((rows, columns), bf16),
            jax.ShapeDtypeStruct((kept, rows, width), bf16),
            jax.ShapeDtypeStruct((given, rows, width), bf16),
            jax.ShapeDtypeStruct((plen, width), bf16),
        ],
        compiler_params=pltpu.CompilerParams(vmem_limit_bytes=56 * 1024 * 1024),
        cost_estimate=pl.CostEstimate(
            flops=10 * rows * columns * pairs,
            bytes_accessed=12 * 1024 * 1024,
            transcendentals=rows * columns * pairs // HD,
        ),
    )(me.astype(jnp.int32)[None], q_rows, grad_rows, kv, kv, prompt, prompt, q_start[None])


def added(*parts):
    total = parts[0].astype(jnp.float32)
    for part in parts[1:]:
        total = total + part.astype(jnp.float32)
    return total.astype(jnp.bfloat16)


def gradients_home(keep, give, me_seq):
    n = lax.axis_size("seq")
    rows = keep.shape[1]
    cut = rows // 2
    odd = jnp.mod(me_seq, 2) == 1
    got = lax.ppermute(give, "seq", [(i, i ^ 1) for i in range(n)])
    none = jnp.zeros_like(got[:1])
    sums = added(
        jnp.concatenate([keep, none]),
        jnp.where(odd, jnp.concatenate([none, got]), jnp.concatenate([got, none])),
    )
    own, one, two, three = sums[0], sums[1], sums[2], sums[3]
    back = lax.ppermute(two[:cut], "seq", [(i, i - 2) for i in range(4, n)])
    ahead = lax.ppermute(two[cut:], "seq", [(i, (i + 2) % n) for i in range(4, n)])
    zero = jnp.zeros_like(back)
    one = added(one, jnp.concatenate([back, zero]))
    three = added(three, jnp.concatenate([zero, ahead]))
    from_next = lax.ppermute(one, "seq", [(i, i - 2) for i in range(2, n)])
    from_last = lax.ppermute(three, "seq", [(i, (i + 2) % n) for i in (n - 2, n - 1, 0, 1)])
    return added(own, from_next, from_last)


def on_device(queries, resp_kv, prompt_kv, d_out, resp_lengths, prompt_home):
    q_rows = queries[0]
    own_kv = resp_kv[0]
    own_prompt = prompt_kv[0]
    grad_rows = d_out[0]
    rows = q_rows.shape[0]
    n_seq = lax.axis_size("seq")
    n_dp = lax.axis_size("dp")
    span = 5 * n_seq // 8
    me_seq = lax.axis_index("seq")
    me_dp = lax.axis_index("dp")
    offset = jnp.mod(me_dp - prompt_home[0], n_dp)

    kv = lax.all_gather(own_kv, "seq", axis=0, tiled=True)

    window = own_prompt[None]
    reach = 1
    while reach < SPREAD:
        window = jnp.concatenate([window, passed_along(window, "dp", reach)], axis=0)
        reach *= 2
    chosen = lax.dynamic_index_in_dim(window, offset, 0, keepdims=False)
    prompt = lax.all_gather(chosen, "seq", axis=0, tiled=True)

    lengths = resp_lengths[0]
    starts = jnp.cumsum(lengths) - lengths
    q_ids = me_seq * rows + jnp.arange(rows, dtype=jnp.int32)
    q_start = jnp.max(jnp.where(starts[None, :] <= q_ids[:, None], starts[None, :], 0), axis=1)
    d_query, keep, give, d_prompt = attend(
        q_rows, grad_rows, kv, prompt, q_start, me_seq, span
    )
    prompt_grad = lax.psum_scatter(d_prompt, "seq", scatter_dimension=0, tiled=True)
    d_kv = gradients_home(keep, give, me_seq)

    slots = jnp.arange(SPREAD, dtype=jnp.int32)[:, None, None]
    held = jnp.where(slots == offset, prompt_grad[None], jnp.zeros((), prompt_grad.dtype))
    reach = SPREAD // 2
    while reach > 0:
        arrived = passed_along(held[reach:], "dp", -reach)
        held = (held[:reach].astype(jnp.float32) + arrived.astype(jnp.float32)).astype(held.dtype)
        reach //= 2
    return (d_query[None], d_kv[None], held)


def solution(mesh):
    placed = (
        P("dp", "seq", None),
        P("dp", "seq", None),
        P("dp", "seq", None),
        P("dp", "seq", None),
        P("dp", None),
        P("dp"),
    )
    return jax.shard_map(
        on_device,
        mesh=mesh,
        in_specs=placed,
        out_specs=(P("dp", "seq", None), P("dp", "seq", None), P("dp", "seq", None)),
        check_vma=False,
    )
```

```python
import functools

import jax
import jax.numpy as jnp
from jax import lax
from jax.experimental import pallas as pl
from jax.experimental.pallas import tpu as pltpu
from jax.sharding import PartitionSpec as P

KVH = 8
HD = 128
SPREAD = 8
NEG = -1e30
LOG2E = 1.4426950408889634


def passed_along(value, axis, by):
    peers = lax.axis_size(axis)
    return lax.ppermute(value, axis, [(i, (i + by) % peers) for i in range(peers)])


def stacked(block):
    heads = block.shape[1] // HD
    return jnp.concatenate([block[:, h * HD : (h + 1) * HD] for h in range(heads)], axis=0)


def attention_kernel(span, n_seq, info, q_ref, g_ref, start_ref, *refs):
    key_refs, value_refs = refs[:8], refs[8:16]
    dq_ref, keep_ref, give_ref, pkeep_ref, bias = refs[16:]
    rows = q_ref.shape[0]
    heads = q_ref.shape[1] // HD
    slot = key_refs[0].shape[0]
    plen = slot * n_seq
    odd = lax.rem(info[0], 2) == 1
    half = KVH * HD
    window = (span + 1) * rows
    scale = HD ** -0.5
    me = info[0]
    head = pl.program_id(0)

    @pl.when(head == 0)
    def _():
        own = me * rows
        k_ids = own - span * rows + lax.broadcasted_iota(jnp.int32, (window, rows), 0)
        q_ids = own + lax.broadcasted_iota(jnp.int32, (window, rows), 1)
        seen = (k_ids >= start_ref[...]) & (k_ids <= q_ids)
        bias[...] = jnp.where(seen, 0.0, NEG)

    def laid_out(refs):
        mine, across, last, next_, own, two, got_near, got_far = [ref[...] for ref in refs]
        cut = rows // 2
        far = cut + slot
        four = [last[:cut], next_[:cut]]
        other4 = jnp.concatenate([got_far[:cut], got_far[far : far + cut]], axis=0)
        other3 = got_near[rows:]
        blocks = [mine, last[cut:], across, next_[cut:]]
        blocks += [got_far[2 * far : 2 * far + slot], got_far[cut:far]]
        blocks += [got_far[2 * far + slot :], got_far[far + cut : 2 * far]]
        blocks += [jnp.where(odd, other4, other3), *four, jnp.where(odd, other3, other4)]
        blocks += [two, got_near[:rows], own]
        return jnp.concatenate(blocks, axis=0)

    keys = laid_out(key_refs)
    values = laid_out(value_refs)
    q_rows = stacked(q_ref[...])
    g_rows = stacked(g_ref[...])
    nt = (((1,), (1,)), ((), ()))
    nn = (((1,), (0,)), ((), ()))
    tn = (((0,), (0,)), ((), ()))
    scores = lax.dot_general(keys, q_rows, nt, preferred_element_type=jnp.float32)
    shade = jnp.concatenate([bias[...]] * heads, axis=1)
    scores = jnp.concatenate([scores[:plen], scores[plen:] + shade], axis=0)
    top = jnp.max(scores, axis=0, keepdims=True)
    expo = jnp.exp2((scores - top) * (scale * LOG2E))
    weights = expo * (1.0 / jnp.sum(expo, axis=0, keepdims=True))
    d_weights = lax.dot_general(values, g_rows, nt, preferred_element_type=jnp.float32)
    delta = jnp.sum(weights * d_weights, axis=0, keepdims=True)
    d_scores = (weights * (d_weights - delta)).astype(jnp.bfloat16)
    weights_b = weights.astype(jnp.bfloat16)
    d_value = lax.dot_general(weights_b, g_rows, nn, preferred_element_type=jnp.float32)
    d_key = lax.dot_general(d_scores, q_rows, nn, preferred_element_type=jnp.float32) * scale
    d_query = lax.dot_general(d_scores, keys, tn, preferred_element_type=jnp.float32) * scale
    d_query = d_query.astype(jnp.bfloat16)
    for h in range(heads):
        dq_ref[:, h * HD : (h + 1) * HD] = d_query[h * rows : (h + 1) * rows]
    given = (span + 1) // 2 * rows
    for part, base in ((d_key, 0), (d_value, half)):
        part = part.astype(jnp.bfloat16)
        columns = pl.ds(pl.multiple_of(base + head * HD, HD), HD)
        for back in range(span + 1):
            block = part[plen + (span - back) * rows : plen + (span - back + 1) * rows]
            if back % 2 == 0:
                keep_ref[back // 2, :, columns] = block
            else:
                give_ref[back // 2 * rows : (back // 2 + 1) * rows, columns] = block
        pkeep_ref[:, columns] = part[: plen // 2]
        give_ref[given:, columns] = part[plen // 2 : plen]


def attend(q_rows, grad_rows, kv, q_start, me, span, n_seq):
    rows, columns = q_rows.shape
    plen, width = n_seq * kv[0].shape[0], kv[0].shape[1]
    group = columns // KVH
    bf16 = jnp.bfloat16
    at = lambda n, col: pl.BlockSpec((n, col), lambda g, s: (0, g))
    later = lambda n: pl.BlockSpec((n, HD), lambda g, s: (0, KVH + g))
    pairs = (span + 1) * rows + plen
    kept, given = span // 2 + 1, (span + 1) // 2
    return pl.pallas_call(
        functools.partial(attention_kernel, span, n_seq),
        grid_spec=pltpu.PrefetchScalarGridSpec(
            num_scalar_prefetch=1,
            grid=(KVH,),
            in_specs=[
                at(rows, group),
                at(rows, group),
                pl.BlockSpec((1, rows), lambda g, s: (0, 0)),
            ]
            + [at(x.shape[0], HD) for x in kv]
            + [later(x.shape[0]) for x in kv],
            out_specs=[
                at(rows, group),
                pl.BlockSpec((kept, rows, width), lambda g, s: (0, 0, 0)),
                pl.BlockSpec((given * rows + plen // 2, width), lambda g, s: (0, 0)),
                pl.BlockSpec((plen // 2, width), lambda g, s: (0, 0)),
            ],
            scratch_shapes=[pltpu.VMEM(((span + 1) * rows, rows), jnp.float32)],
        ),
        out_shape=[
            jax.ShapeDtypeStruct((rows, columns), bf16),
            jax.ShapeDtypeStruct((kept, rows, width), bf16),
            jax.ShapeDtypeStruct((given * rows + plen // 2, width), bf16),
            jax.ShapeDtypeStruct((plen // 2, width), bf16),
        ],
        compiler_params=pltpu.CompilerParams(vmem_limit_bytes=56 * 1024 * 1024),
        cost_estimate=pl.CostEstimate(
            flops=10 * rows * columns * pairs,
            bytes_accessed=12 * 1024 * 1024,
            transcendentals=rows * columns * pairs // HD,
        ),
    )(me.astype(jnp.int32)[None], q_rows, grad_rows, q_start[None], *kv, *kv)


def added(*parts):
    total = parts[0].astype(jnp.float32)
    for part in parts[1:]:
        total = total + part.astype(jnp.float32)
    return total.astype(jnp.bfloat16)


def along_seq(value, pairs):
    return lax.ppermute(value, "seq", pairs)


def rounds_in(own, prompt, offset, odd):
    n = lax.axis_size("seq")
    cut = own.shape[0] // 2
    behind = [(i, (i - 2) % n) for i in range(n)]
    ahead = [(i, (i + 2) % n) for i in range(n)]
    across = [(i, (i + 4) % n) for i in range(n)]
    swap = [(i, i ^ 1) for i in range(n)]
    tied = lax.optimization_barrier

    by1 = passed_along(prompt, "dp", 1)
    pair = jnp.concatenate([prompt, by1])
    pair, own = tied((pair, own))
    two = along_seq(own, [(i, i + 2) for i in range(n - 2)])
    six = along_seq(own, [(i, (i - 2) % n) for i in range(4)])
    pairs = [passed_along(pair, "dp", step) for step in range(2, SPREAD, 2)]
    *pairs, two, six = tied((*pairs, two, six))
    top2, low6 = two[:cut], six[cut:]

    window = jnp.concatenate([pair, *pairs])
    chosen = lax.dynamic_index_in_dim(window, offset, 0, keepdims=False)
    from_last = along_seq(jnp.concatenate([top2, chosen]), ahead)
    from_next = along_seq(jnp.concatenate([low6, chosen]), behind)
    from_across = along_seq(chosen, across)
    near = jnp.concatenate([jnp.where(odd, two, own), jnp.where(odd, six, two)])
    got_near = along_seq(near, swap)
    from_last, from_next, from_across, chosen, got_near = tied(
        (from_last, from_next, from_across, chosen, got_near)
    )
    got_far = along_seq(jnp.concatenate([from_last, from_next, chosen, from_across]), swap)
    return [chosen, from_across, from_last, from_next, own, two, got_near, got_far]


def rounds_out(keep, give, pkeep, offset):
    n = lax.axis_size("seq")
    rows = keep.shape[1]
    cut = rows // 2
    slot = pkeep.shape[0] // (n // 2)
    behind = [(i, (i - 2) % n) for i in range(n)]
    ahead = [(i, (i + 2) % n) for i in range(n)]
    across = [(i, (i + 4) % n) for i in range(n)]
    swap = [(i, i ^ 1) for i in range(n)]
    tied = lax.optimization_barrier
    me = lax.axis_index("seq")
    odd = jnp.mod(me, 2) == 1

    got = along_seq(give, swap)
    got, pgot = got[: -pkeep.shape[0]].reshape((-1,) + keep.shape[1:]), got[-pkeep.shape[0] :]
    none = jnp.zeros_like(got[:1])
    sums = added(
        jnp.concatenate([keep, none]),
        jnp.where(odd, jnp.concatenate([none, got]), jnp.concatenate([got, none])),
    )
    own, one, two, three = sums[0], sums[1], sums[2], sums[3]
    prompt = added(pkeep, pgot)
    mine, to_behind, to_across, to_ahead = [prompt[i * slot : (i + 1) * slot] for i in range(4)]

    from_next = along_seq(jnp.concatenate([two[:cut], to_behind]), behind)
    from_last = along_seq(jnp.concatenate([two[cut:], to_ahead]), ahead)
    from_across = along_seq(to_across, across)
    from_next, from_last, from_across, one, three = tied(
        (from_next, from_last, from_across, one, three)
    )

    prompt = added(mine, from_next[cut:], from_last[cut:], from_across)
    none = jnp.zeros((), prompt.dtype)
    left = [jnp.where(offset == i, prompt, none) for i in range(SPREAD)]
    zero = jnp.zeros_like(prompt, shape=(cut,) + prompt.shape[1:])
    passing = (me >= n - 2) | (me < 2)
    one = added(one, jnp.concatenate([from_next[:cut], zero]))
    three = added(
        three, jnp.concatenate([zero, jnp.where(passing, from_last[:cut], none)])
    )
    from_next = along_seq(one, [(i, i - 2) for i in range(2, n)])
    from_last = along_seq(three, [(i, (i + 2) % n) for i in (n - 2, n - 1, 0, 1)])
    pairs = [
        passed_along(jnp.stack(left[step : step + 2]), "dp", -step)
        for step in range(2, SPREAD, 2)
    ]
    *pairs, from_next, from_last = tied((*pairs, from_next, from_last))
    by1 = passed_along(added(left[1], *[pair[1] for pair in pairs]), "dp", -1)
    d_kv = added(own, from_next, from_last)
    return d_kv, added(left[0], by1, *[pair[0] for pair in pairs])


def on_device(queries, resp_kv, prompt_kv, d_out, resp_lengths, prompt_home):
    q_rows = queries[0]
    own_kv = resp_kv[0]
    grad_rows = d_out[0]
    rows = q_rows.shape[0]
    n_seq = lax.axis_size("seq")
    n_dp = lax.axis_size("dp")
    span = 5 * n_seq // 8
    me_seq = lax.axis_index("seq")
    me_dp = lax.axis_index("dp")
    odd = jnp.mod(me_seq, 2) == 1
    offset = jnp.mod(me_dp - prompt_home[0], n_dp)

    kv = rounds_in(own_kv, prompt_kv, offset, odd)

    lengths = resp_lengths[0]
    starts = jnp.cumsum(lengths) - lengths
    q_ids = me_seq * rows + jnp.arange(rows, dtype=jnp.int32)
    q_start = jnp.max(jnp.where(starts[None, :] <= q_ids[:, None], starts[None, :], 0), axis=1)
    d_query, keep, give, pkeep = attend(
        q_rows, grad_rows, kv, q_start, me_seq, span, n_seq
    )
    d_kv, d_prompt = rounds_out(keep, give, pkeep, offset)
    return (d_query[None], d_kv[None], d_prompt[None])


def solution(mesh):
    placed = (
        P("dp", "seq", None),
        P("dp", "seq", None),
        P("dp", "seq", None),
        P("dp", "seq", None),
        P("dp", None),
        P("dp"),
    )
    return jax.shard_map(
        on_device,
        mesh=mesh,
        in_specs=placed,
        out_specs=(P("dp", "seq", None), P("dp", "seq", None), P("dp", "seq", None)),
        check_vma=False,
    )
```

```python
import functools

import jax
import jax.numpy as jnp
from jax import lax
from jax.experimental import pallas as pl
from jax.experimental.pallas import tpu as pltpu
from jax.sharding import PartitionSpec as P

KVH = 8
HD = 128
SPREAD = 8
NEG = -1e30
LOG2E = 1.4426950408889634


def passed_along(value, axis, by):
    peers = lax.axis_size(axis)
    return lax.ppermute(value, axis, [(i, (i + by) % peers) for i in range(peers)])


def stacked(block):
    heads = block.shape[1] // HD
    return jnp.concatenate([block[:, h * HD : (h + 1) * HD] for h in range(heads)], axis=0)


def attention_kernel(span, n_seq, info, q_ref, g_ref, k_ref, v_ref, pk_ref, pv_ref, start_ref,
                     dq_ref, dkv_ref, pkeep_ref, pgive_ref, bias):
    rows = q_ref.shape[0]
    heads = q_ref.shape[1] // HD
    plen = pk_ref.shape[0]
    half = KVH * HD
    window = (span + 1) * rows
    scale = HD ** -0.5
    me = info[0]
    head = pl.program_id(0)
    slot = plen // n_seq
    chips = n_seq // 2
    chip = lax.div(me, 2)
    odd = lax.rem(me, 2) == 1

    @pl.when(head == 0)
    def _():
        own = me * rows
        k_ids = own - span * rows + lax.broadcasted_iota(jnp.int32, (window, rows), 0)
        q_ids = own + lax.broadcasted_iota(jnp.int32, (window, rows), 1)
        seen = (k_ids >= start_ref[...]) & (k_ids <= q_ids)
        bias[...] = jnp.where(seen, 0.0, NEG)
        dkv_ref[...] = jnp.zeros_like(dkv_ref)

    near = [
        pl.ds(pl.multiple_of(jnp.maximum(me - back, 0) * rows, rows), rows)
        for back in range(span, -1, -1)
    ]
    keys = jnp.concatenate([pk_ref[...]] + [k_ref[at, :] for at in near], axis=0)
    values = jnp.concatenate([pv_ref[...]] + [v_ref[at, :] for at in near], axis=0)
    q_rows = stacked(q_ref[...])
    g_rows = stacked(g_ref[...])
    nt = (((1,), (1,)), ((), ()))
    nn = (((1,), (0,)), ((), ()))
    tn = (((0,), (0,)), ((), ()))
    scores = lax.dot_general(keys, q_rows, nt, preferred_element_type=jnp.float32)
    shade = jnp.concatenate([bias[...]] * heads, axis=1)
    scores = jnp.concatenate([scores[:plen], scores[plen:] + shade], axis=0)
    top = jnp.max(scores, axis=0, keepdims=True)
    expo = jnp.exp2((scores - top) * (scale * LOG2E))
    weights = expo * (1.0 / jnp.sum(expo, axis=0, keepdims=True))
    d_weights = lax.dot_general(values, g_rows, nt, preferred_element_type=jnp.float32)
    delta = jnp.sum(weights * d_weights, axis=0, keepdims=True)
    d_scores = (weights * (d_weights - delta)).astype(jnp.bfloat16)
    weights_b = weights.astype(jnp.bfloat16)
    d_value = lax.dot_general(weights_b, g_rows, nn, preferred_element_type=jnp.float32)
    d_key = lax.dot_general(d_scores, q_rows, nn, preferred_element_type=jnp.float32) * scale
    d_query = lax.dot_general(d_scores, keys, tn, preferred_element_type=jnp.float32) * scale
    d_query = d_query.astype(jnp.bfloat16)
    for h in range(heads):
        dq_ref[:, h * HD : (h + 1) * HD] = d_query[h * rows : (h + 1) * rows]
    for part, base in ((d_key, 0), (d_value, half)):
        part = part.astype(jnp.bfloat16)
        columns = pl.ds(pl.multiple_of(base + head * HD, HD), HD)
        for i, at in enumerate(near):
            dkv_ref[at, columns] = part[plen + i * rows : plen + (i + 1) * rows]
        for c in range(chips):
            first = part[2 * c * slot : (2 * c + 1) * slot]
            second = part[(2 * c + 1) * slot : (2 * c + 2) * slot]
            back = pl.multiple_of(lax.rem(chip - c + chips, chips) * slot, slot)
            pkeep_ref[pl.ds(back, slot), columns] = jnp.where(odd, second, first)
            pgive_ref[pl.ds(back, slot), columns] = jnp.where(odd, first, second)


def attend(q_rows, grad_rows, kv, prompt, q_start, me, span, n_seq):
    rows, columns = q_rows.shape
    total, width = kv.shape
    plen = prompt.shape[0]
    group = columns // KVH
    bf16 = jnp.bfloat16
    at = lambda n, col: pl.BlockSpec((n, col), lambda g, s: (0, g))
    later = lambda n: pl.BlockSpec((n, HD), lambda g, s: (0, KVH + g))
    pairs = (span + 1) * rows + plen
    return pl.pallas_call(
        functools.partial(attention_kernel, span, n_seq),
        grid_spec=pltpu.PrefetchScalarGridSpec(
            num_scalar_prefetch=1,
            grid=(KVH,),
            in_specs=[
                at(rows, group),
                at(rows, group),
                at(total, HD),
                later(total),
                at(plen, HD),
                later(plen),
                pl.BlockSpec((1, rows), lambda g, s: (0, 0)),
            ],
            out_specs=[
                at(rows, group),
                pl.BlockSpec((total, width), lambda g, s: (0, 0)),
                pl.BlockSpec((plen // 2, width), lambda g, s: (0, 0)),
                pl.BlockSpec((plen // 2, width), lambda g, s: (0, 0)),
            ],
            scratch_shapes=[pltpu.VMEM(((span + 1) * rows, rows), jnp.float32)],
        ),
        out_shape=[
            jax.ShapeDtypeStruct((rows, columns), bf16),
            jax.ShapeDtypeStruct((total, width), bf16),
            jax.ShapeDtypeStruct((plen // 2, width), bf16),
            jax.ShapeDtypeStruct((plen // 2, width), bf16),
        ],
        compiler_params=pltpu.CompilerParams(vmem_limit_bytes=56 * 1024 * 1024),
        cost_estimate=pl.CostEstimate(
            flops=10 * rows * columns * pairs,
            bytes_accessed=12 * 1024 * 1024,
            transcendentals=rows * columns * pairs // HD,
        ),
    )(me.astype(jnp.int32)[None], q_rows, grad_rows, kv, kv, prompt, prompt, q_start[None])


def added(*parts):
    total = parts[0].astype(jnp.float32)
    for part in parts[1:]:
        total = total + part.astype(jnp.float32)
    return total.astype(jnp.bfloat16)


def added(*parts):
    total = parts[0].astype(jnp.float32)
    for part in parts[1:]:
        total = total + part.astype(jnp.float32)
    return total.astype(jnp.bfloat16)


def along_seq(value, pairs):
    return lax.ppermute(value, "seq", pairs)


def prompt_for(prompt, offset):
    by1 = passed_along(prompt, "dp", 1)
    pair = jnp.concatenate([prompt, by1])
    pairs = [passed_along(pair, "dp", step) for step in range(2, SPREAD, 2)]
    window = jnp.concatenate([pair, *pairs])
    chosen = lax.dynamic_index_in_dim(window, offset, 0, keepdims=False)
    return lax.all_gather(chosen, "seq", axis=0, tiled=True)


def prompt_home_sum(keep, give, offset):
    n = lax.axis_size("seq")
    slot = keep.shape[0] // (n // 2)
    total = added(keep, along_seq(give, [(i, i ^ 1) for i in range(n)]))
    mine, to_behind, to_across, to_ahead = [total[i * slot : (i + 1) * slot] for i in range(4)]
    parts = [
        along_seq(to_across, [(i, (i + 4) % n) for i in range(n)]),
        along_seq(to_behind, [(i, (i - 2) % n) for i in range(n)]),
        along_seq(to_ahead, [(i, (i + 2) % n) for i in range(n)]),
    ]
    total = added(mine, *parts)
    left = [jnp.where(offset == i, total, jnp.zeros((), total.dtype)) for i in range(SPREAD)]
    pairs = [
        passed_along(jnp.stack(left[step : step + 2]), "dp", -step)
        for step in range(2, SPREAD, 2)
    ]
    by1 = passed_along(added(left[1], *[pair[1] for pair in pairs]), "dp", -1)
    return added(left[0], by1, *[pair[0] for pair in pairs])


def on_device(queries, resp_kv, prompt_kv, d_out, resp_lengths, prompt_home):
    q_rows = queries[0]
    own_kv = resp_kv[0]
    grad_rows = d_out[0]
    rows = q_rows.shape[0]
    n_seq = lax.axis_size("seq")
    n_dp = lax.axis_size("dp")
    span = 5 * n_seq // 8
    me_seq = lax.axis_index("seq")
    me_dp = lax.axis_index("dp")
    offset = jnp.mod(me_dp - prompt_home[0], n_dp)

    kv = lax.all_gather(own_kv, "seq", axis=0, tiled=True)
    prompt = prompt_for(prompt_kv, offset)

    lengths = resp_lengths[0]
    starts = jnp.cumsum(lengths) - lengths
    q_ids = me_seq * rows + jnp.arange(rows, dtype=jnp.int32)
    q_start = jnp.max(jnp.where(starts[None, :] <= q_ids[:, None], starts[None, :], 0), axis=1)
    d_query, d_near, keep, give = attend(
        q_rows, grad_rows, kv, prompt, q_start, me_seq, span, n_seq
    )
    d_kv = lax.psum_scatter(d_near, "seq", scatter_dimension=0, tiled=True)
    d_prompt = prompt_home_sum(keep, give, offset)
    return (d_query[None], d_kv[None], d_prompt[None])


def solution(mesh):
    placed = (
        P("dp", "seq", None),
        P("dp", "seq", None),
        P("dp", "seq", None),
        P("dp", "seq", None),
        P("dp", None),
        P("dp"),
    )
    return jax.shard_map(
        on_device,
        mesh=mesh,
        in_specs=placed,
        out_specs=(P("dp", "seq", None), P("dp", "seq", None), P("dp", "seq", None)),
        check_vma=False,
    )
```

```python
import functools

import jax
import jax.numpy as jnp
from jax import lax
from jax.experimental import pallas as pl
from jax.experimental.pallas import tpu as pltpu
from jax.sharding import PartitionSpec as P

KVH = 8
HD = 128
SPREAD = 8
NEG = -1e30
LOG2E = 1.4426950408889634


def passed_along(value, axis, by):
    peers = lax.axis_size(axis)
    return lax.ppermute(value, axis, [(i, (i + by) % peers) for i in range(peers)])


def stacked(block):
    heads = block.shape[1] // HD
    return jnp.concatenate([block[:, h * HD : (h + 1) * HD] for h in range(heads)], axis=0)


def attention_kernel(span, n_seq, info, q_ref, g_ref, start_ref, *refs):
    key_refs, value_refs = refs[:8], refs[8:16]
    dq_ref, keep_ref, give_ref, pkeep_ref, bias = refs[16:]
    rows = q_ref.shape[0]
    heads = q_ref.shape[1] // HD
    slot = key_refs[0].shape[0]
    plen = slot * n_seq
    odd = lax.rem(info[0], 2) == 1
    half = KVH * HD
    window = (span + 1) * rows
    scale = HD ** -0.5
    me = info[0]
    head = pl.program_id(0)

    @pl.when(head == 0)
    def _():
        own = me * rows
        k_ids = own - span * rows + lax.broadcasted_iota(jnp.int32, (window, rows), 0)
        q_ids = own + lax.broadcasted_iota(jnp.int32, (window, rows), 1)
        seen = (k_ids >= start_ref[...]) & (k_ids <= q_ids)
        bias[...] = jnp.where(seen, 0.0, NEG)

    def laid_out(refs):
        mine, across, last, next_, own, two, got_near, got_far = [ref[...] for ref in refs]
        cut = rows // 2
        far = cut + slot
        four = [last[:cut], next_[:cut]]
        other4 = jnp.concatenate([got_far[:cut], got_far[far : far + cut]], axis=0)
        other3 = got_near[rows:]
        blocks = [mine, last[cut:], across, next_[cut:]]
        blocks += [got_far[2 * far : 2 * far + slot], got_far[cut:far]]
        blocks += [got_far[2 * far + slot :], got_far[far + cut : 2 * far]]
        blocks += [jnp.where(odd, other4, other3), *four, jnp.where(odd, other3, other4)]
        blocks += [two, got_near[:rows], own]
        return jnp.concatenate(blocks, axis=0)

    keys = laid_out(key_refs)
    values = laid_out(value_refs)
    q_rows = stacked(q_ref[...])
    g_rows = stacked(g_ref[...])
    nt = (((1,), (1,)), ((), ()))
    nn = (((1,), (0,)), ((), ()))
    tn = (((0,), (0,)), ((), ()))
    scores = lax.dot_general(keys, q_rows, nt, preferred_element_type=jnp.float32)
    shade = jnp.concatenate([bias[...]] * heads, axis=1)
    scores = jnp.concatenate([scores[:plen], scores[plen:] + shade], axis=0)
    top = jnp.max(scores, axis=0, keepdims=True)
    expo = jnp.exp2((scores - top) * (scale * LOG2E))
    weights = expo * (1.0 / jnp.sum(expo, axis=0, keepdims=True))
    d_weights = lax.dot_general(values, g_rows, nt, preferred_element_type=jnp.float32)
    delta = jnp.sum(weights * d_weights, axis=0, keepdims=True)
    d_scores = (weights * (d_weights - delta)).astype(jnp.bfloat16)
    weights_b = weights.astype(jnp.bfloat16)
    d_value = lax.dot_general(weights_b, g_rows, nn, preferred_element_type=jnp.float32)
    d_key = lax.dot_general(d_scores, q_rows, nn, preferred_element_type=jnp.float32) * scale
    d_query = lax.dot_general(d_scores, keys, tn, preferred_element_type=jnp.float32) * scale
    d_query = d_query.astype(jnp.bfloat16)
    for h in range(heads):
        dq_ref[:, h * HD : (h + 1) * HD] = d_query[h * rows : (h + 1) * rows]
    given = (span + 1) // 2 * rows
    for part, base in ((d_key, 0), (d_value, half)):
        part = part.astype(jnp.bfloat16)
        columns = pl.ds(pl.multiple_of(base + head * HD, HD), HD)
        for back in range(span + 1):
            block = part[plen + (span - back) * rows : plen + (span - back + 1) * rows]
            if back % 2 == 0:
                keep_ref[back // 2, :, columns] = block
            else:
                give_ref[back // 2 * rows : (back // 2 + 1) * rows, columns] = block
        pkeep_ref[:, columns] = part[: plen // 2]
        give_ref[given:, columns] = part[plen // 2 : plen]


def attend(q_rows, grad_rows, kv, q_start, me, span, n_seq):
    rows, columns = q_rows.shape
    plen, width = n_seq * kv[0].shape[0], kv[0].shape[1]
    group = columns // KVH
    bf16 = jnp.bfloat16
    at = lambda n, col: pl.BlockSpec((n, col), lambda g, s: (0, g))
    later = lambda n: pl.BlockSpec((n, HD), lambda g, s: (0, KVH + g))
    pairs = (span + 1) * rows + plen
    kept, given = span // 2 + 1, (span + 1) // 2
    return pl.pallas_call(
        functools.partial(attention_kernel, span, n_seq),
        grid_spec=pltpu.PrefetchScalarGridSpec(
            num_scalar_prefetch=1,
            grid=(KVH,),
            in_specs=[
                at(rows, group),
                at(rows, group),
                pl.BlockSpec((1, rows), lambda g, s: (0, 0)),
            ]
            + [at(x.shape[0], HD) for x in kv]
            + [later(x.shape[0]) for x in kv],
            out_specs=[
                at(rows, group),
                pl.BlockSpec((kept, rows, width), lambda g, s: (0, 0, 0)),
                pl.BlockSpec((given * rows + plen // 2, width), lambda g, s: (0, 0)),
                pl.BlockSpec((plen // 2, width), lambda g, s: (0, 0)),
            ],
            scratch_shapes=[pltpu.VMEM(((span + 1) * rows, rows), jnp.float32)],
        ),
        out_shape=[
            jax.ShapeDtypeStruct((rows, columns), bf16),
            jax.ShapeDtypeStruct((kept, rows, width), bf16),
            jax.ShapeDtypeStruct((given * rows + plen // 2, width), bf16),
            jax.ShapeDtypeStruct((plen // 2, width), bf16),
        ],
        compiler_params=pltpu.CompilerParams(vmem_limit_bytes=56 * 1024 * 1024),
        cost_estimate=pl.CostEstimate(
            flops=10 * rows * columns * pairs,
            bytes_accessed=12 * 1024 * 1024,
            transcendentals=rows * columns * pairs // HD,
        ),
    )(me.astype(jnp.int32)[None], q_rows, grad_rows, q_start[None], *kv, *kv)


def added(*parts):
    total = parts[0].astype(jnp.float32)
    for part in parts[1:]:
        total = total + part.astype(jnp.float32)
    return total.astype(jnp.bfloat16)


def along_seq(value, pairs):
    return lax.ppermute(value, "seq", pairs)


def rounds_in(own, prompt, offset, odd):
    n = lax.axis_size("seq")
    cut = own.shape[0] // 2
    behind = [(i, (i - 2) % n) for i in range(n)]
    ahead = [(i, (i + 2) % n) for i in range(n)]
    across = [(i, (i + 4) % n) for i in range(n)]
    swap = [(i, i ^ 1) for i in range(n)]
    tied = lax.optimization_barrier

    by1 = passed_along(prompt, "dp", 1)
    top2 = along_seq(own[:cut], [(i, i + 2) for i in range(n - 2)])
    low6 = along_seq(own[cut:], [(i, (i - 2) % n) for i in range(4)])
    low, top2 = tied((own[cut:], top2))
    top, low6 = tied((own[:cut], low6))
    low2 = along_seq(low, [(i, i + 2) for i in range(n - 2)])
    top6 = along_seq(top, [(1, n - 1)])
    pair = jnp.concatenate([prompt, by1])
    pairs = [passed_along(pair, "dp", step) for step in range(2, SPREAD, 2)]
    *pairs, top2, low6 = tied((*pairs, top2, low6))

    window = jnp.concatenate([pair, *pairs])
    chosen = lax.dynamic_index_in_dim(window, offset, 0, keepdims=False)
    from_last = along_seq(jnp.concatenate([top2, chosen]), ahead)
    from_next = along_seq(jnp.concatenate([low6, chosen]), behind)
    from_across = along_seq(chosen, across)
    two = jnp.concatenate([top2, low2])
    six = jnp.concatenate([top6, low6])
    near = jnp.concatenate([jnp.where(odd, two, own), jnp.where(odd, six, two)])
    got_near = along_seq(near, swap)
    got_far = along_seq(jnp.concatenate([from_last, from_next, chosen, from_across]), swap)
    return [chosen, from_across, from_last, from_next, own, two, got_near, got_far]


def rounds_out(keep, give, pkeep, offset):
    n = lax.axis_size("seq")
    rows = keep.shape[1]
    cut = rows // 2
    slot = pkeep.shape[0] // (n // 2)
    behind = [(i, (i - 2) % n) for i in range(n)]
    ahead = [(i, (i + 2) % n) for i in range(n)]
    across = [(i, (i + 4) % n) for i in range(n)]
    swap = [(i, i ^ 1) for i in range(n)]
    tied = lax.optimization_barrier
    me = lax.axis_index("seq")
    odd = jnp.mod(me, 2) == 1

    got = along_seq(give, swap)
    got, pgot = got[: -pkeep.shape[0]].reshape((-1,) + keep.shape[1:]), got[-pkeep.shape[0] :]
    none = jnp.zeros_like(got[:1])
    sums = added(
        jnp.concatenate([keep, none]),
        jnp.where(odd, jnp.concatenate([none, got]), jnp.concatenate([got, none])),
    )
    own, one, two, three = sums[0], sums[1], sums[2], sums[3]
    prompt = added(pkeep, pgot)
    mine, to_behind, to_across, to_ahead = [prompt[i * slot : (i + 1) * slot] for i in range(4)]

    from_next = along_seq(jnp.concatenate([two[:cut], to_behind]), behind)
    from_last = along_seq(jnp.concatenate([two[cut:], to_ahead]), ahead)
    from_across = along_seq(to_across, across)
    low1 = along_seq(one[cut:], [(i, i - 2) for i in range(2, n)])
    top3 = along_seq(three[:cut], [(n - 1, 1)])
    from_next, from_last, from_across = tied((from_next, from_last, from_across))

    prompt = added(mine, from_next[cut:], from_last[cut:], from_across)
    none = jnp.zeros((), prompt.dtype)
    left = [jnp.where(offset == i, prompt, none) for i in range(SPREAD)]
    passing = (me >= n - 2) | (me < 2)
    top_one = added(one[:cut], from_next[:cut])
    low_three = added(three[cut:], jnp.where(passing, from_last[:cut], none))
    top_one, low_three, low1, top3 = tied((top_one, low_three, low1, top3))
    pairs = [
        passed_along(jnp.stack(left[step : step + 2]), "dp", -step)
        for step in range(2, SPREAD, 2)
    ]
    top1 = along_seq(top_one, [(i, i - 2) for i in range(2, n)])
    low3 = along_seq(low_three, [(i, (i + 2) % n) for i in (n - 2, n - 1, 0, 1)])
    *pairs, top1, low3 = tied((*pairs, top1, low3))
    by1 = passed_along(added(left[1], *[pair[1] for pair in pairs]), "dp", -1)
    d_kv = added(own, jnp.concatenate([top1, low1]), jnp.concatenate([top3, low3]))
    return d_kv, added(left[0], by1, *[pair[0] for pair in pairs])


def on_device(queries, resp_kv, prompt_kv, d_out, resp_lengths, prompt_home):
    q_rows = queries[0]
    own_kv = resp_kv[0]
    grad_rows = d_out[0]
    rows = q_rows.shape[0]
    n_seq = lax.axis_size("seq")
    n_dp = lax.axis_size("dp")
    span = 5 * n_seq // 8
    me_seq = lax.axis_index("seq")
    me_dp = lax.axis_index("dp")
    odd = jnp.mod(me_seq, 2) == 1
    offset = jnp.mod(me_dp - prompt_home[0], n_dp)

    kv = rounds_in(own_kv, prompt_kv, offset, odd)

    lengths = resp_lengths[0]
    starts = jnp.cumsum(lengths) - lengths
    q_ids = me_seq * rows + jnp.arange(rows, dtype=jnp.int32)
    q_start = jnp.max(jnp.where(starts[None, :] <= q_ids[:, None], starts[None, :], 0), axis=1)
    d_query, keep, give, pkeep = attend(
        q_rows, grad_rows, kv, q_start, me_seq, span, n_seq
    )
    d_kv, d_prompt = rounds_out(keep, give, pkeep, offset)
    return (d_query[None], d_kv[None], d_prompt[None])


def solution(mesh):
    placed = (
        P("dp", "seq", None),
        P("dp", "seq", None),
        P("dp", "seq", None),
        P("dp", "seq", None),
        P("dp", None),
        P("dp"),
    )
    return jax.shard_map(
        on_device,
        mesh=mesh,
        in_specs=placed,
        out_specs=(P("dp", "seq", None), P("dp", "seq", None), P("dp", "seq", None)),
        check_vma=False,
    )
```

```python
import functools

import jax
import jax.numpy as jnp
from jax import lax
from jax.experimental import pallas as pl
from jax.experimental.pallas import tpu as pltpu
from jax.sharding import PartitionSpec as P

KVH = 8
HD = 128
SPREAD = 8
NEG = -1e30
UNIT = 2
LOG2E = 1.4426950408889634


def passed_along(value, axis, by):
    peers = lax.axis_size(axis)
    return lax.ppermute(value, axis, [(i, (i + by) % peers) for i in range(peers)])


def stacked(block):
    heads = block.shape[1] // HD
    return jnp.concatenate([block[:, h * HD : (h + 1) * HD] for h in range(heads)], axis=0)


def attention_kernel(span, n_seq, info, q_ref, g_ref, start_ref, *refs):
    key_refs, value_refs = refs[:8], refs[8:16]
    dq_ref, keep_ref, give_ref, pkeep_ref, bias = refs[16:]
    rows = q_ref.shape[0]
    heads = q_ref.shape[1] // HD // UNIT
    slot = key_refs[0].shape[0]
    plen = slot * n_seq
    odd = lax.rem(info[0], 2) == 1
    half = KVH * HD
    window = (span + 1) * rows
    scale = HD ** -0.5
    me = info[0]
    head = pl.program_id(0)

    @pl.when(head == 0)
    def _():
        own = me * rows
        k_ids = own - span * rows + lax.broadcasted_iota(jnp.int32, (window, rows), 0)
        q_ids = own + lax.broadcasted_iota(jnp.int32, (window, rows), 1)
        seen = (k_ids >= start_ref[...]) & (k_ids <= q_ids)
        bias[...] = jnp.where(seen, 0.0, NEG)

    def one(u):
        def laid_out(refs):
            mine, across, last, next_, own, two, got_near, got_far = [ref[:, u * HD : (u + 1) * HD] for ref in refs]
            cut = rows // 2
            far = cut + slot
            four = [last[:cut], next_[:cut]]
            other4 = jnp.concatenate([got_far[:cut], got_far[far : far + cut]], axis=0)
            other3 = got_near[rows:]
            blocks = [mine, last[cut:], across, next_[cut:]]
            blocks += [got_far[2 * far : 2 * far + slot], got_far[cut:far]]
            blocks += [got_far[2 * far + slot :], got_far[far + cut : 2 * far]]
            blocks += [jnp.where(odd, other4, other3), *four, jnp.where(odd, other3, other4)]
            blocks += [two, got_near[:rows], own]
            return jnp.concatenate(blocks, axis=0)

        keys = laid_out(key_refs)
        values = laid_out(value_refs)
        q_rows = stacked(q_ref[:, u * heads * HD : (u + 1) * heads * HD])
        g_rows = stacked(g_ref[:, u * heads * HD : (u + 1) * heads * HD])
        nt = (((1,), (1,)), ((), ()))
        nn = (((1,), (0,)), ((), ()))
        tn = (((0,), (0,)), ((), ()))
        scores = lax.dot_general(keys, q_rows, nt, preferred_element_type=jnp.float32)
        shade = jnp.concatenate([bias[...]] * heads, axis=1)
        scores = jnp.concatenate([scores[:plen], scores[plen:] + shade], axis=0)
        top = jnp.max(scores, axis=0, keepdims=True)
        expo = jnp.exp2((scores - top) * (scale * LOG2E))
        weights = expo * (1.0 / jnp.sum(expo, axis=0, keepdims=True))
        d_weights = lax.dot_general(values, g_rows, nt, preferred_element_type=jnp.float32)
        delta = jnp.sum(weights * d_weights, axis=0, keepdims=True)
        d_scores = (weights * (d_weights - delta)).astype(jnp.bfloat16)
        weights_b = weights.astype(jnp.bfloat16)
        d_value = lax.dot_general(weights_b, g_rows, nn, preferred_element_type=jnp.float32)
        d_key = lax.dot_general(d_scores, q_rows, nn, preferred_element_type=jnp.float32) * scale
        d_query = lax.dot_general(d_scores, keys, tn, preferred_element_type=jnp.float32) * scale
        d_query = d_query.astype(jnp.bfloat16)
        for h in range(heads):
            dq_ref[:, (u * heads + h) * HD : (u * heads + h + 1) * HD] = d_query[h * rows : (h + 1) * rows]
        given = (span + 1) // 2 * rows
        for part, base in ((d_key, 0), (d_value, half)):
            part = part.astype(jnp.bfloat16)
            columns = pl.ds(pl.multiple_of(base + (head * UNIT + u) * HD, HD), HD)
            for back in range(span + 1):
                block = part[plen + (span - back) * rows : plen + (span - back + 1) * rows]
                if back % 2 == 0:
                    keep_ref[back // 2, :, columns] = block
                else:
                    give_ref[back // 2 * rows : (back // 2 + 1) * rows, columns] = block
            pkeep_ref[:, columns] = part[: plen // 2]
            give_ref[given:, columns] = part[plen // 2 : plen]

    for u in range(UNIT):
        one(u)


def attend(q_rows, grad_rows, kv, q_start, me, span, n_seq):
    rows, columns = q_rows.shape
    plen, width = n_seq * kv[0].shape[0], kv[0].shape[1]
    group = columns // KVH * UNIT
    bf16 = jnp.bfloat16
    at = lambda n, col: pl.BlockSpec((n, col), lambda g, s: (0, g))
    later = lambda n: pl.BlockSpec((n, UNIT * HD), lambda g, s: (0, KVH // UNIT + g))
    pairs = (span + 1) * rows + plen
    kept, given = span // 2 + 1, (span + 1) // 2
    return pl.pallas_call(
        functools.partial(attention_kernel, span, n_seq),
        grid_spec=pltpu.PrefetchScalarGridSpec(
            num_scalar_prefetch=1,
            grid=(KVH // UNIT,),
            in_specs=[
                at(rows, group),
                at(rows, group),
                pl.BlockSpec((1, rows), lambda g, s: (0, 0)),
            ]
            + [at(x.shape[0], UNIT * HD) for x in kv]
            + [later(x.shape[0]) for x in kv],
            out_specs=[
                at(rows, group),
                pl.BlockSpec((kept, rows, width), lambda g, s: (0, 0, 0)),
                pl.BlockSpec((given * rows + plen // 2, width), lambda g, s: (0, 0)),
                pl.BlockSpec((plen // 2, width), lambda g, s: (0, 0)),
            ],
            scratch_shapes=[pltpu.VMEM(((span + 1) * rows, rows), jnp.float32)],
        ),
        out_shape=[
            jax.ShapeDtypeStruct((rows, columns), bf16),
            jax.ShapeDtypeStruct((kept, rows, width), bf16),
            jax.ShapeDtypeStruct((given * rows + plen // 2, width), bf16),
            jax.ShapeDtypeStruct((plen // 2, width), bf16),
        ],
        compiler_params=pltpu.CompilerParams(vmem_limit_bytes=56 * 1024 * 1024),
        cost_estimate=pl.CostEstimate(
            flops=10 * rows * columns * pairs,
            bytes_accessed=12 * 1024 * 1024,
            transcendentals=rows * columns * pairs // HD,
        ),
    )(me.astype(jnp.int32)[None], q_rows, grad_rows, q_start[None], *kv, *kv)


def added(*parts):
    total = parts[0].astype(jnp.float32)
    for part in parts[1:]:
        total = total + part.astype(jnp.float32)
    return total.astype(jnp.bfloat16)


def along_seq(value, pairs):
    return lax.ppermute(value, "seq", pairs)


def rounds_in(own, prompt, offset, odd):
    n = lax.axis_size("seq")
    cut = own.shape[0] // 2
    behind = [(i, (i - 2) % n) for i in range(n)]
    ahead = [(i, (i + 2) % n) for i in range(n)]
    across = [(i, (i + 4) % n) for i in range(n)]
    swap = [(i, i ^ 1) for i in range(n)]
    tied = lax.optimization_barrier

    by1 = passed_along(prompt, "dp", 1)
    top2 = along_seq(own[:cut], [(i, i + 2) for i in range(n - 2)])
    low6 = along_seq(own[cut:], [(i, (i - 2) % n) for i in range(4)])
    low, top2 = tied((own[cut:], top2))
    top, low6 = tied((own[:cut], low6))
    low2 = along_seq(low, [(i, i + 2) for i in range(n - 2)])
    top6 = along_seq(top, [(1, n - 1)])
    pair = jnp.concatenate([prompt, by1])
    pairs = [passed_along(pair, "dp", step) for step in range(2, SPREAD, 2)]
    *pairs, top2, low6 = tied((*pairs, top2, low6))

    window = jnp.concatenate([pair, *pairs])
    chosen = lax.dynamic_index_in_dim(window, offset, 0, keepdims=False)
    from_last = along_seq(jnp.concatenate([top2, chosen]), ahead)
    from_next = along_seq(jnp.concatenate([low6, chosen]), behind)
    from_across = along_seq(chosen, across)
    two = jnp.concatenate([top2, low2])
    six = jnp.concatenate([top6, low6])
    near = jnp.concatenate([jnp.where(odd, two, own), jnp.where(odd, six, two)])
    got_near = along_seq(near, swap)
    got_far = along_seq(jnp.concatenate([from_last, from_next, chosen, from_across]), swap)
    return [chosen, from_across, from_last, from_next, own, two, got_near, got_far]


def rounds_out(keep, give, pkeep, offset):
    n = lax.axis_size("seq")
    rows = keep.shape[1]
    cut = rows // 2
    slot = pkeep.shape[0] // (n // 2)
    behind = [(i, (i - 2) % n) for i in range(n)]
    ahead = [(i, (i + 2) % n) for i in range(n)]
    across = [(i, (i + 4) % n) for i in range(n)]
    swap = [(i, i ^ 1) for i in range(n)]
    tied = lax.optimization_barrier
    me = lax.axis_index("seq")
    odd = jnp.mod(me, 2) == 1

    got = along_seq(give, swap)
    got, pgot = got[: -pkeep.shape[0]].reshape((-1,) + keep.shape[1:]), got[-pkeep.shape[0] :]
    none = jnp.zeros_like(got[:1])
    sums = added(
        jnp.concatenate([keep, none]),
        jnp.where(odd, jnp.concatenate([none, got]), jnp.concatenate([got, none])),
    )
    own, one, two, three = sums[0], sums[1], sums[2], sums[3]
    prompt = added(pkeep, pgot)
    mine, to_behind, to_across, to_ahead = [prompt[i * slot : (i + 1) * slot] for i in range(4)]

    from_next = along_seq(jnp.concatenate([two[:cut], to_behind]), behind)
    from_last = along_seq(jnp.concatenate([two[cut:], to_ahead]), ahead)
    from_across = along_seq(to_across, across)
    low1 = along_seq(one[cut:], [(i, i - 2) for i in range(2, n)])
    top3 = along_seq(three[:cut], [(n - 1, 1)])
    from_next, from_last, from_across = tied((from_next, from_last, from_across))

    prompt = added(mine, from_next[cut:], from_last[cut:], from_across)
    none = jnp.zeros((), prompt.dtype)
    left = [jnp.where(offset == i, prompt, none) for i in range(SPREAD)]
    passing = (me >= n - 2) | (me < 2)
    top_one = added(one[:cut], from_next[:cut])
    low_three = added(three[cut:], jnp.where(passing, from_last[:cut], none))
    stacks = [jnp.stack(left[step : step + 2]) for step in range(2, SPREAD, 2)]
    pairs = [passed_along(x, "dp", -step) for x, step in zip(stacks, range(2, SPREAD, 2))]
    top_one, low_three, low1, top3, pairs[0] = tied((top_one, low_three, low1, top3, pairs[0]))
    top1 = along_seq(top_one, [(i, i - 2) for i in range(2, n)])
    low3 = along_seq(low_three, [(i, (i + 2) % n) for i in (n - 2, n - 1, 0, 1)])
    *pairs, top1, low3 = tied((*pairs, top1, low3))
    by1 = passed_along(added(left[1], *[pair[1] for pair in pairs]), "dp", -1)
    d_kv = added(own, jnp.concatenate([top1, low1]), jnp.concatenate([top3, low3]))
    return d_kv, added(left[0], by1, *[pair[0] for pair in pairs])


def on_device(queries, resp_kv, prompt_kv, d_out, resp_lengths, prompt_home):
    q_rows = queries[0]
    own_kv = resp_kv[0]
    grad_rows = d_out[0]
    rows = q_rows.shape[0]
    n_seq = lax.axis_size("seq")
    n_dp = lax.axis_size("dp")
    span = 5 * n_seq // 8
    me_seq = lax.axis_index("seq")
    me_dp = lax.axis_index("dp")
    odd = jnp.mod(me_seq, 2) == 1
    offset = jnp.mod(me_dp - prompt_home[0], n_dp)

    kv = rounds_in(own_kv, prompt_kv, offset, odd)

    lengths = resp_lengths[0]
    starts = jnp.cumsum(lengths) - lengths
    q_ids = me_seq * rows + jnp.arange(rows, dtype=jnp.int32)
    q_start = jnp.max(jnp.where(starts[None, :] <= q_ids[:, None], starts[None, :], 0), axis=1)
    d_query, keep, give, pkeep = attend(
        q_rows, grad_rows, kv, q_start, me_seq, span, n_seq
    )
    d_kv, d_prompt = rounds_out(keep, give, pkeep, offset)
    return (d_query[None], d_kv[None], d_prompt[None])


def solution(mesh):
    placed = (
        P("dp", "seq", None),
        P("dp", "seq", None),
        P("dp", "seq", None),
        P("dp", "seq", None),
        P("dp", None),
        P("dp"),
    )
    return jax.shard_map(
        on_device,
        mesh=mesh,
        in_specs=placed,
        out_specs=(P("dp", "seq", None), P("dp", "seq", None), P("dp", "seq", None)),
        check_vma=False,
    )
```

```python
import functools

import jax
import jax.numpy as jnp
from jax import lax
from jax.experimental import pallas as pl
from jax.experimental.pallas import tpu as pltpu
from jax.sharding import PartitionSpec as P

KVH = 8
HD = 128
SPREAD = 8
NEG = -1e30
UNIT = 2
LOG2E = 1.4426950408889634


def passed_along(value, axis, by):
    peers = lax.axis_size(axis)
    return lax.ppermute(value, axis, [(i, (i + by) % peers) for i in range(peers)])


def stacked(block):
    heads = block.shape[1] // HD
    return jnp.concatenate([block[:, h * HD : (h + 1) * HD] for h in range(heads)], axis=0)


def attention_kernel(span, n_seq, info, q_ref, g_ref, start_ref, *refs):
    key_refs, value_refs = refs[:8], refs[8:16]
    dq_ref, keep_ref, give_ref, pkeep_ref, bias = refs[16:]
    rows = q_ref.shape[0]
    heads = q_ref.shape[1] // HD // UNIT
    slot = key_refs[0].shape[0]
    plen = slot * n_seq
    odd = lax.rem(info[0], 2) == 1
    half = KVH * HD
    window = (span + 1) * rows
    scale = HD ** -0.5
    me = info[0]
    head = pl.program_id(0)

    @pl.when(head == 0)
    def _():
        own = me * rows
        k_ids = own - span * rows + lax.broadcasted_iota(jnp.int32, (window, rows), 0)
        q_ids = own + lax.broadcasted_iota(jnp.int32, (window, rows), 1)
        seen = (k_ids >= start_ref[...]) & (k_ids <= q_ids)
        bias[...] = jnp.where(seen, 0.0, NEG)

    def one(u):
        def laid_out(refs):
            mine, across, last, next_, own, two, got_near, got_far = [ref[:, u * HD : (u + 1) * HD] for ref in refs]
            cut = rows // 2
            far = cut + slot
            four = [last[:cut], next_[:cut]]
            other4 = jnp.concatenate([got_far[:cut], got_far[far : far + cut]], axis=0)
            other3 = got_near[rows:]
            blocks = [mine, last[cut:], across, next_[cut:]]
            blocks += [got_far[2 * far : 2 * far + slot], got_far[cut:far]]
            blocks += [got_far[2 * far + slot :], got_far[far + cut : 2 * far]]
            blocks += [jnp.where(odd, other4, other3), *four, jnp.where(odd, other3, other4)]
            blocks += [two, got_near[:rows], own]
            return jnp.concatenate(blocks, axis=0)

        keys = laid_out(key_refs)
        values = laid_out(value_refs)
        q_rows = stacked(q_ref[:, u * heads * HD : (u + 1) * heads * HD])
        g_rows = stacked(g_ref[:, u * heads * HD : (u + 1) * heads * HD])
        nt = (((1,), (1,)), ((), ()))
        nn = (((1,), (0,)), ((), ()))
        tn = (((0,), (0,)), ((), ()))
        scores = lax.dot_general(keys, q_rows, nt, preferred_element_type=jnp.float32)
        shade = jnp.concatenate([bias[...]] * heads, axis=1)
        scores = jnp.concatenate([scores[:plen], scores[plen:] + shade], axis=0)
        top = jnp.max(scores, axis=0, keepdims=True)
        expo = jnp.exp2((scores - top) * (scale * LOG2E))
        weights = expo * (1.0 / jnp.sum(expo, axis=0, keepdims=True))
        d_weights = lax.dot_general(values, g_rows, nt, preferred_element_type=jnp.float32)
        delta = jnp.sum(weights * d_weights, axis=0, keepdims=True)
        d_scores = (weights * (d_weights - delta)).astype(jnp.bfloat16)
        weights_b = weights.astype(jnp.bfloat16)
        d_value = lax.dot_general(weights_b, g_rows, nn, preferred_element_type=jnp.float32)
        d_key = lax.dot_general(d_scores, q_rows, nn, preferred_element_type=jnp.float32) * scale
        d_query = lax.dot_general(d_scores, keys, tn, preferred_element_type=jnp.float32) * scale
        d_query = d_query.astype(jnp.bfloat16)
        for h in range(heads):
            dq_ref[:, (u * heads + h) * HD : (u * heads + h + 1) * HD] = d_query[h * rows : (h + 1) * rows]
        given = (span + 1) // 2 * rows
        for part, base in ((d_key, 0), (d_value, half)):
            part = part.astype(jnp.bfloat16)
            columns = pl.ds(pl.multiple_of(base + (head * UNIT + u) * HD, HD), HD)
            for back in range(span + 1):
                block = part[plen + (span - back) * rows : plen + (span - back + 1) * rows]
                if back % 2 == 0:
                    keep_ref[back // 2, :, columns] = block
                else:
                    give_ref[back // 2 * rows : (back // 2 + 1) * rows, columns] = block
            pkeep_ref[:, columns] = part[: plen // 2]
            give_ref[given:, columns] = part[plen // 2 : plen]

    for u in range(UNIT):
        one(u)


def attend(q_rows, grad_rows, kv, q_start, me, span, n_seq):
    rows, columns = q_rows.shape
    plen, width = n_seq * kv[0].shape[0], kv[0].shape[1]
    group = columns // KVH * UNIT
    bf16 = jnp.bfloat16
    at = lambda n, col: pl.BlockSpec((n, col), lambda g, s: (0, g))
    later = lambda n: pl.BlockSpec((n, UNIT * HD), lambda g, s: (0, KVH // UNIT + g))
    pairs = (span + 1) * rows + plen
    kept, given = span // 2 + 1, (span + 1) // 2
    return pl.pallas_call(
        functools.partial(attention_kernel, span, n_seq),
        grid_spec=pltpu.PrefetchScalarGridSpec(
            num_scalar_prefetch=1,
            grid=(KVH // UNIT,),
            in_specs=[
                at(rows, group),
                at(rows, group),
                pl.BlockSpec((1, rows), lambda g, s: (0, 0)),
            ]
            + [at(x.shape[0], UNIT * HD) for x in kv]
            + [later(x.shape[0]) for x in kv],
            out_specs=[
                at(rows, group),
                pl.BlockSpec((kept, rows, width), lambda g, s: (0, 0, 0)),
                pl.BlockSpec((given * rows + plen // 2, width), lambda g, s: (0, 0)),
                pl.BlockSpec((plen // 2, width), lambda g, s: (0, 0)),
            ],
            scratch_shapes=[pltpu.VMEM(((span + 1) * rows, rows), jnp.float32)],
        ),
        out_shape=[
            jax.ShapeDtypeStruct((rows, columns), bf16),
            jax.ShapeDtypeStruct((kept, rows, width), bf16),
            jax.ShapeDtypeStruct((given * rows + plen // 2, width), bf16),
            jax.ShapeDtypeStruct((plen // 2, width), bf16),
        ],
        compiler_params=pltpu.CompilerParams(vmem_limit_bytes=56 * 1024 * 1024),
        cost_estimate=pl.CostEstimate(
            flops=10 * rows * columns * pairs,
            bytes_accessed=12 * 1024 * 1024,
            transcendentals=rows * columns * pairs // HD,
        ),
    )(me.astype(jnp.int32)[None], q_rows, grad_rows, q_start[None], *kv, *kv)


def added(*parts):
    total = parts[0].astype(jnp.float32)
    for part in parts[1:]:
        total = total + part.astype(jnp.float32)
    return total.astype(jnp.bfloat16)


def along_seq(value, pairs):
    return lax.ppermute(value, "seq", pairs)


def rounds_in(own, prompt, offset, odd):
    n = lax.axis_size("seq")
    cut = own.shape[0] // 2
    behind = [(i, (i - 2) % n) for i in range(n)]
    ahead = [(i, (i + 2) % n) for i in range(n)]
    across = [(i, (i + 4) % n) for i in range(n)]
    swap = [(i, i ^ 1) for i in range(n)]
    tied = lax.optimization_barrier

    by1 = passed_along(prompt, "dp", 1)
    top2 = along_seq(own[:cut], [(i, i + 2) for i in range(n - 2)])
    low6 = along_seq(own[cut:], [(i, (i - 2) % n) for i in range(4)])
    low, top2 = tied((own[cut:], top2))
    top, low6 = tied((own[:cut], low6))
    low2 = along_seq(low, [(i, i + 2) for i in range(n - 2)])
    top6 = along_seq(top, [(1, n - 1)])
    pair = jnp.concatenate([prompt, by1])
    pairs = [passed_along(pair, "dp", step) for step in range(2, SPREAD, 2)]
    *pairs, top2, low6 = tied((*pairs, top2, low6))

    window = jnp.concatenate([pair, *pairs])
    chosen = lax.dynamic_index_in_dim(window, offset, 0, keepdims=False)
    from_last = along_seq(jnp.concatenate([top2, chosen]), ahead)
    from_next = along_seq(jnp.concatenate([low6, chosen]), behind)
    from_across = along_seq(chosen, across)
    two = jnp.concatenate([top2, low2])
    six = jnp.concatenate([top6, low6])
    near = jnp.concatenate([jnp.where(odd, two, own), jnp.where(odd, six, two)])
    got_near = along_seq(near, swap)
    got_far = along_seq(jnp.concatenate([from_last, from_next, chosen, from_across]), swap)
    return [chosen, from_across, from_last, from_next, own, two, got_near, got_far]


def rounds_out(keep, give, pkeep, offset):
    n = lax.axis_size("seq")
    rows = keep.shape[1]
    cut = rows // 2
    slot = pkeep.shape[0] // (n // 2)
    behind = [(i, (i - 2) % n) for i in range(n)]
    ahead = [(i, (i + 2) % n) for i in range(n)]
    across = [(i, (i + 4) % n) for i in range(n)]
    swap = [(i, i ^ 1) for i in range(n)]
    tied = lax.optimization_barrier
    me = lax.axis_index("seq")
    odd = jnp.mod(me, 2) == 1

    got = along_seq(give, swap)
    got, pgot = got[: -pkeep.shape[0]].reshape((-1,) + keep.shape[1:]), got[-pkeep.shape[0] :]
    none = jnp.zeros_like(got[:1])
    sums = added(
        jnp.concatenate([keep, none]),
        jnp.where(odd, jnp.concatenate([none, got]), jnp.concatenate([got, none])),
    )
    own, one, two, three = sums[0], sums[1], sums[2], sums[3]
    prompt = added(pkeep, pgot)
    mine, to_behind, to_across, to_ahead = [prompt[i * slot : (i + 1) * slot] for i in range(4)]

    from_next = along_seq(jnp.concatenate([two[:cut], to_behind]), behind)
    from_last = along_seq(jnp.concatenate([two[cut:], to_ahead]), ahead)
    from_across = along_seq(to_across, across)
    low1 = along_seq(one[cut:], [(i, i - 2) for i in range(2, n)])
    top3 = along_seq(three[:cut], [(n - 1, 1)])
    from_next, from_last, from_across = tied((from_next, from_last, from_across))

    prompt = added(mine, from_next[cut:], from_last[cut:], from_across)
    none = jnp.zeros((), prompt.dtype)
    left = [jnp.where(offset == i, prompt, none) for i in range(SPREAD)]
    passing = (me >= n - 2) | (me < 2)
    top_one = added(one[:cut], from_next[:cut])
    low_three = added(three[cut:], jnp.where(passing, from_last[:cut], none))
    stacks = [jnp.stack(left[step : step + 2]) for step in range(2, SPREAD, 2)]
    pairs = [passed_along(x, "dp", -step) for x, step in zip(stacks, range(2, SPREAD, 2))]
    top_one, low_three, low1, top3, pairs[0] = tied((top_one, low_three, low1, top3, pairs[0]))
    top1 = along_seq(top_one, [(i, i - 2) for i in range(2, n)])
    low3 = along_seq(low_three, [(i, (i + 2) % n) for i in (n - 2, n - 1, 0, 1)])
    by1 = passed_along(added(left[1], *[pair[1] for pair in pairs]), "dp", -1)
    d_kv = added(own, jnp.concatenate([top1, low1]), jnp.concatenate([top3, low3]))
    return d_kv, added(left[0], by1, *[pair[0] for pair in pairs])


def on_device(queries, resp_kv, prompt_kv, d_out, resp_lengths, prompt_home):
    q_rows = queries[0]
    own_kv = resp_kv[0]
    grad_rows = d_out[0]
    rows = q_rows.shape[0]
    n_seq = lax.axis_size("seq")
    n_dp = lax.axis_size("dp")
    span = 5 * n_seq // 8
    me_seq = lax.axis_index("seq")
    me_dp = lax.axis_index("dp")
    odd = jnp.mod(me_seq, 2) == 1
    offset = jnp.mod(me_dp - prompt_home[0], n_dp)

    kv = rounds_in(own_kv, prompt_kv, offset, odd)

    lengths = resp_lengths[0]
    starts = jnp.cumsum(lengths) - lengths
    q_ids = me_seq * rows + jnp.arange(rows, dtype=jnp.int32)
    q_start = jnp.max(jnp.where(starts[None, :] <= q_ids[:, None], starts[None, :], 0), axis=1)
    d_query, keep, give, pkeep = attend(
        q_rows, grad_rows, kv, q_start, me_seq, span, n_seq
    )
    d_kv, d_prompt = rounds_out(keep, give, pkeep, offset)
    return (d_query[None], d_kv[None], d_prompt[None])


def solution(mesh):
    placed = (
        P("dp", "seq", None),
        P("dp", "seq", None),
        P("dp", "seq", None),
        P("dp", "seq", None),
        P("dp", None),
        P("dp"),
    )
    return jax.shard_map(
        on_device,
        mesh=mesh,
        in_specs=placed,
        out_specs=(P("dp", "seq", None), P("dp", "seq", None), P("dp", "seq", None)),
        check_vma=False,
    )
```

```python
import functools

import jax
import jax.numpy as jnp
from jax import lax
from jax.experimental import pallas as pl
from jax.experimental.pallas import tpu as pltpu
from jax.sharding import PartitionSpec as P

KVH = 8
HD = 128
SPREAD = 8
NEG = -1e30
UNIT = 4
LOG2E = 1.4426950408889634


def passed_along(value, axis, by):
    peers = lax.axis_size(axis)
    return lax.ppermute(value, axis, [(i, (i + by) % peers) for i in range(peers)])


def stacked(block):
    heads = block.shape[1] // HD
    return jnp.concatenate([block[:, h * HD : (h + 1) * HD] for h in range(heads)], axis=0)


def attention_kernel(span, n_seq, info, q_ref, g_ref, start_ref, *refs):
    key_refs, value_refs = refs[:8], refs[8:16]
    dq_ref, keep_ref, give_ref, pkeep_ref, bias = refs[16:]
    rows = q_ref.shape[0]
    heads = q_ref.shape[1] // HD // UNIT
    slot = key_refs[0].shape[0]
    plen = slot * n_seq
    odd = lax.rem(info[0], 2) == 1
    half = KVH * HD
    window = (span + 1) * rows
    scale = HD ** -0.5
    me = info[0]
    head = pl.program_id(0)

    @pl.when(head == 0)
    def _():
        own = me * rows
        k_ids = own - span * rows + lax.broadcasted_iota(jnp.int32, (window, rows), 0)
        q_ids = own + lax.broadcasted_iota(jnp.int32, (window, rows), 1)
        seen = (k_ids >= start_ref[...]) & (k_ids <= q_ids)
        bias[...] = jnp.where(seen, 0.0, NEG)

    def one(u):
        def laid_out(refs):
            mine, across, last, next_, own, two, got_near, got_far = [ref[:, u * HD : (u + 1) * HD] for ref in refs]
            cut = rows // 2
            far = cut + slot
            four = [last[:cut], next_[:cut]]
            other4 = jnp.concatenate([got_far[:cut], got_far[far : far + cut]], axis=0)
            other3 = got_near[rows:]
            blocks = [mine, last[cut:], across, next_[cut:]]
            blocks += [got_far[2 * far : 2 * far + slot], got_far[cut:far]]
            blocks += [got_far[2 * far + slot :], got_far[far + cut : 2 * far]]
            blocks += [jnp.where(odd, other4, other3), *four, jnp.where(odd, other3, other4)]
            blocks += [two, got_near[:rows], own]
            return jnp.concatenate(blocks, axis=0)

        keys = laid_out(key_refs)
        values = laid_out(value_refs)
        q_rows = stacked(q_ref[:, u * heads * HD : (u + 1) * heads * HD])
        g_rows = stacked(g_ref[:, u * heads * HD : (u + 1) * heads * HD])
        nt = (((1,), (1,)), ((), ()))
        nn = (((1,), (0,)), ((), ()))
        tn = (((0,), (0,)), ((), ()))
        scores = lax.dot_general(keys, q_rows, nt, preferred_element_type=jnp.float32)
        shade = jnp.concatenate([bias[...]] * heads, axis=1)
        scores = jnp.concatenate([scores[:plen], scores[plen:] + shade], axis=0)
        top = jnp.max(scores, axis=0, keepdims=True)
        expo = jnp.exp2((scores - top) * (scale * LOG2E))
        weights = expo * (1.0 / jnp.sum(expo, axis=0, keepdims=True))
        d_weights = lax.dot_general(values, g_rows, nt, preferred_element_type=jnp.float32)
        delta = jnp.sum(weights * d_weights, axis=0, keepdims=True)
        d_scores = (weights * (d_weights - delta)).astype(jnp.bfloat16)
        weights_b = weights.astype(jnp.bfloat16)
        d_value = lax.dot_general(weights_b, g_rows, nn, preferred_element_type=jnp.float32)
        d_key = lax.dot_general(d_scores, q_rows, nn, preferred_element_type=jnp.float32) * scale
        d_query = lax.dot_general(d_scores, keys, tn, preferred_element_type=jnp.float32) * scale
        d_query = d_query.astype(jnp.bfloat16)
        for h in range(heads):
            dq_ref[:, (u * heads + h) * HD : (u * heads + h + 1) * HD] = d_query[h * rows : (h + 1) * rows]
        given = (span + 1) // 2 * rows
        for part, base in ((d_key, 0), (d_value, half)):
            part = part.astype(jnp.bfloat16)
            columns = pl.ds(pl.multiple_of(base + (head * UNIT + u) * HD, HD), HD)
            for back in range(span + 1):
                block = part[plen + (span - back) * rows : plen + (span - back + 1) * rows]
                if back % 2 == 0:
                    keep_ref[back // 2, :, columns] = block
                else:
                    give_ref[back // 2 * rows : (back // 2 + 1) * rows, columns] = block
            pkeep_ref[:, columns] = part[: plen // 2]
            give_ref[given:, columns] = part[plen // 2 : plen]

    for u in range(UNIT):
        one(u)


def attend(q_rows, grad_rows, kv, q_start, me, span, n_seq):
    rows, columns = q_rows.shape
    plen, width = n_seq * kv[0].shape[0], kv[0].shape[1]
    group = columns // KVH * UNIT
    bf16 = jnp.bfloat16
    at = lambda n, col: pl.BlockSpec((n, col), lambda g, s: (0, g))
    later = lambda n: pl.BlockSpec((n, UNIT * HD), lambda g, s: (0, KVH // UNIT + g))
    pairs = (span + 1) * rows + plen
    kept, given = span // 2 + 1, (span + 1) // 2
    return pl.pallas_call(
        functools.partial(attention_kernel, span, n_seq),
        grid_spec=pltpu.PrefetchScalarGridSpec(
            num_scalar_prefetch=1,
            grid=(KVH // UNIT,),
            in_specs=[
                at(rows, group),
                at(rows, group),
                pl.BlockSpec((1, rows), lambda g, s: (0, 0)),
            ]
            + [at(x.shape[0], UNIT * HD) for x in kv]
            + [later(x.shape[0]) for x in kv],
            out_specs=[
                at(rows, group),
                pl.BlockSpec((kept, rows, width), lambda g, s: (0, 0, 0)),
                pl.BlockSpec((given * rows + plen // 2, width), lambda g, s: (0, 0)),
                pl.BlockSpec((plen // 2, width), lambda g, s: (0, 0)),
            ],
            scratch_shapes=[pltpu.VMEM(((span + 1) * rows, rows), jnp.float32)],
        ),
        out_shape=[
            jax.ShapeDtypeStruct((rows, columns), bf16),
            jax.ShapeDtypeStruct((kept, rows, width), bf16),
            jax.ShapeDtypeStruct((given * rows + plen // 2, width), bf16),
            jax.ShapeDtypeStruct((plen // 2, width), bf16),
        ],
        compiler_params=pltpu.CompilerParams(vmem_limit_bytes=56 * 1024 * 1024),
        cost_estimate=pl.CostEstimate(
            flops=10 * rows * columns * pairs,
            bytes_accessed=12 * 1024 * 1024,
            transcendentals=rows * columns * pairs // HD,
        ),
    )(me.astype(jnp.int32)[None], q_rows, grad_rows, q_start[None], *kv, *kv)


def added(*parts):
    total = parts[0].astype(jnp.float32)
    for part in parts[1:]:
        total = total + part.astype(jnp.float32)
    return total.astype(jnp.bfloat16)


def along_seq(value, pairs):
    return lax.ppermute(value, "seq", pairs)


def rounds_in(own, prompt, offset, odd):
    n = lax.axis_size("seq")
    cut = own.shape[0] // 2
    behind = [(i, (i - 2) % n) for i in range(n)]
    ahead = [(i, (i + 2) % n) for i in range(n)]
    across = [(i, (i + 4) % n) for i in range(n)]
    swap = [(i, i ^ 1) for i in range(n)]
    tied = lax.optimization_barrier

    by1 = passed_along(prompt, "dp", 1)
    top2 = along_seq(own[:cut], [(i, i + 2) for i in range(n - 2)])
    low6 = along_seq(own[cut:], [(i, (i - 2) % n) for i in range(4)])
    low, top2 = tied((own[cut:], top2))
    top, low6 = tied((own[:cut], low6))
    low2 = along_seq(low, [(i, i + 2) for i in range(n - 2)])
    top6 = along_seq(top, [(1, n - 1)])
    pair = jnp.concatenate([prompt, by1])
    pairs = [passed_along(pair, "dp", step) for step in range(2, SPREAD, 2)]
    *pairs, top2, low6 = tied((*pairs, top2, low6))

    window = jnp.concatenate([pair, *pairs])
    chosen = lax.dynamic_index_in_dim(window, offset, 0, keepdims=False)
    from_last = along_seq(jnp.concatenate([top2, chosen]), ahead)
    from_next = along_seq(jnp.concatenate([low6, chosen]), behind)
    from_across = along_seq(chosen, across)
    two = jnp.concatenate([top2, low2])
    six = jnp.concatenate([top6, low6])
    near = jnp.concatenate([jnp.where(odd, two, own), jnp.where(odd, six, two)])
    got_near = along_seq(near, swap)
    got_far = along_seq(jnp.concatenate([from_last, from_next, chosen, from_across]), swap)
    return [chosen, from_across, from_last, from_next, own, two, got_near, got_far]


def rounds_out(keep, give, pkeep, offset):
    n = lax.axis_size("seq")
    rows = keep.shape[1]
    cut = rows // 2
    slot = pkeep.shape[0] // (n // 2)
    behind = [(i, (i - 2) % n) for i in range(n)]
    ahead = [(i, (i + 2) % n) for i in range(n)]
    across = [(i, (i + 4) % n) for i in range(n)]
    swap = [(i, i ^ 1) for i in range(n)]
    tied = lax.optimization_barrier
    me = lax.axis_index("seq")
    odd = jnp.mod(me, 2) == 1

    got = along_seq(give, swap)
    got, pgot = got[: -pkeep.shape[0]].reshape((-1,) + keep.shape[1:]), got[-pkeep.shape[0] :]
    none = jnp.zeros_like(got[:1])
    sums = added(
        jnp.concatenate([keep, none]),
        jnp.where(odd, jnp.concatenate([none, got]), jnp.concatenate([got, none])),
    )
    own, one, two, three = sums[0], sums[1], sums[2], sums[3]
    prompt = added(pkeep, pgot)
    mine, to_behind, to_across, to_ahead = [prompt[i * slot : (i + 1) * slot] for i in range(4)]

    from_next = along_seq(jnp.concatenate([two[:cut], to_behind]), behind)
    from_last = along_seq(jnp.concatenate([two[cut:], to_ahead]), ahead)
    from_across = along_seq(to_across, across)
    low1 = along_seq(one[cut:], [(i, i - 2) for i in range(2, n)])
    top3 = along_seq(three[:cut], [(n - 1, 1)])
    from_next, from_last, from_across = tied((from_next, from_last, from_across))

    prompt = added(mine, from_next[cut:], from_last[cut:], from_across)
    none = jnp.zeros((), prompt.dtype)
    left = [jnp.where(offset == i, prompt, none) for i in range(SPREAD)]
    passing = (me >= n - 2) | (me < 2)
    top_one = added(one[:cut], from_next[:cut])
    low_three = added(three[cut:], jnp.where(passing, from_last[:cut], none))
    stacks = [jnp.stack(left[step : step + 2]) for step in range(2, SPREAD, 2)]
    pairs = [passed_along(x, "dp", -step) for x, step in zip(stacks, range(2, SPREAD, 2))]
    top_one, low_three, low1, top3, pairs[0] = tied((top_one, low_three, low1, top3, pairs[0]))
    top1 = along_seq(top_one, [(i, i - 2) for i in range(2, n)])
    low3 = along_seq(low_three, [(i, (i + 2) % n) for i in (n - 2, n - 1, 0, 1)])
    by1 = passed_along(added(left[1], *[pair[1] for pair in pairs]), "dp", -1)
    d_kv = added(own, jnp.concatenate([top1, low1]), jnp.concatenate([top3, low3]))
    return d_kv, added(left[0], by1, *[pair[0] for pair in pairs])


def on_device(queries, resp_kv, prompt_kv, d_out, resp_lengths, prompt_home):
    q_rows = queries[0]
    own_kv = resp_kv[0]
    grad_rows = d_out[0]
    rows = q_rows.shape[0]
    n_seq = lax.axis_size("seq")
    n_dp = lax.axis_size("dp")
    span = 5 * n_seq // 8
    me_seq = lax.axis_index("seq")
    me_dp = lax.axis_index("dp")
    odd = jnp.mod(me_seq, 2) == 1
    offset = jnp.mod(me_dp - prompt_home[0], n_dp)

    kv = rounds_in(own_kv, prompt_kv, offset, odd)

    lengths = resp_lengths[0]
    starts = jnp.cumsum(lengths) - lengths
    q_ids = me_seq * rows + jnp.arange(rows, dtype=jnp.int32)
    q_start = jnp.max(jnp.where(starts[None, :] <= q_ids[:, None], starts[None, :], 0), axis=1)
    d_query, keep, give, pkeep = attend(
        q_rows, grad_rows, kv, q_start, me_seq, span, n_seq
    )
    d_kv, d_prompt = rounds_out(keep, give, pkeep, offset)
    return (d_query[None], d_kv[None], d_prompt[None])


def solution(mesh):
    placed = (
        P("dp", "seq", None),
        P("dp", "seq", None),
        P("dp", "seq", None),
        P("dp", "seq", None),
        P("dp", None),
        P("dp"),
    )
    return jax.shard_map(
        on_device,
        mesh=mesh,
        in_specs=placed,
        out_specs=(P("dp", "seq", None), P("dp", "seq", None), P("dp", "seq", None)),
        check_vma=False,
    )
```
